256 devices in a mesh: dp: 4 (over y), region: 64 (over z, x, core).
Axes of the slice: x: 4, y: 4, z: 8, core: 2. Of those that a mesh axis runs over, the one named last changes fastest.
Arguments:
- query: bfloat16 [4, 16384, 1024], P('dp', 'region'), may hold values from -17 to 17
- key_in: bfloat16 [4, 16384, 1024], P('dp', 'region'), may hold values from -17 to 17
- value: bfloat16 [4, 16384, 1024], P('dp', 'region'), may hold values from -6 to 6
- d_out: bfloat16 [4, 16384, 1024], P('dp', 'region'), may hold values from -6 to 6
- out_weight: bfloat16 [1024, 1024], replicated, may hold values from -0.1875 to 0.1875
- attended: int32 [64, 3], P('region'), may hold values from 0 to 63, as said below
- counts: int32 [64], P('region'), may hold values from 2 to 3, as said below
Outputs:
- layer_out: bfloat16 [4, 16384, 1024], P('dp', 'region')
- d_query: bfloat16 [4, 16384, 1024], P('dp', 'region')
- d_key: bfloat16 [4, 16384, 1024], P('dp', 'region')
- d_value: bfloat16 [4, 16384, 1024], P('dp', 'region')
- d_weight: float32 [1024, 1024], P('region')
The draws below stay inside these ranges and needn't reach their ends.
Inputs may be any that keep to these rules, and one draw needn't show every extreme that they name: `attended`: row r starts with r; its next counts[r] - 1 entries are distinct regions among r - 1, r + 1 and one hub region common to all rows (never r itself again); the hub stands in some row whose region is not beside it; entries past counts[r] repeat r. `counts`: some region has 3 in every draw.
All inputs are finite; a program needn't handle non-finite values.
Results may differ from the reference program's by a relative error of at most 0.019.
Values may be sent and summed in bfloat16 or wider, within the bound.
No kernel may reach another device: no remote copies, remote signals or barrier semaphores. Data moves between devices by JAX's collectives and lax.ppermute only.
A program may use at most 128 MiB of HBM per device.

```python
import jax
import jax.numpy as jnp
from jax import lax

D = 1024
HEADS = 16
HEAD_DIM = 64
REGION_TOK = 256
MAXNB = 3
SAMPLES = 4
REGIONS = 64
TOKENS = 16384


def draw_query(key, part):
    key = jax.random.fold_in(key, 1)
    return jnp.clip(jax.random.normal(key, (SAMPLES, TOKENS, D), jnp.float32), -6.0, 6.0).astype(jnp.bfloat16)


def draw_key_in(key, part):
    key = jax.random.fold_in(key, 2)
    return jnp.clip(jax.random.normal(key, (SAMPLES, TOKENS, D), jnp.float32), -6.0, 6.0).astype(jnp.bfloat16)


def hub_pick(key):
    middle = REGIONS // 2
    drawn = jax.random.randint(jax.random.fold_in(key, 11), (), 0, REGIONS - 2)
    return jnp.where(drawn >= middle + 1, drawn + 1, drawn).astype(jnp.int32)


def list_tables(key):
    centre = hub_pick(key)
    middle = REGIONS // 2
    order_key = jax.random.fold_in(key, 7)
    count_key = jax.random.fold_in(key, 8)
    regs = jnp.arange(REGIONS, dtype=jnp.int32)
    options = jnp.stack([regs - 1, regs + 1, jnp.full((REGIONS,), centre, jnp.int32)], axis=1)
    usable = jnp.stack([regs > 0, regs < REGIONS - 1, (centre < regs - 1) | (centre > regs + 1)], axis=1)
    forced = jnp.stack([regs == centre + 1, (regs == middle) | (regs == REGIONS - 2), regs == (centre + middle) % REGIONS], axis=1)
    ranking = jax.random.randint(order_key, (REGIONS, 3), 0, 1000) * 4 + jnp.arange(3, dtype=jnp.int32)[None, :]
    ranking = ranking + jnp.where(usable, 0, 100000) - jnp.where(forced, 50000, 0)
    order = jnp.argsort(ranking, axis=1)
    sorted_options = jnp.take_along_axis(options, order, axis=1)
    usable_count = jnp.sum(usable.astype(jnp.int32), axis=1)
    need = jnp.sum(forced.astype(jnp.int32), axis=1)
    wanted = jax.random.randint(count_key, (REGIONS,), 1, MAXNB)
    extra = jnp.maximum(jnp.minimum(wanted, usable_count), need)
    extra = jnp.where(regs == middle, jnp.minimum(MAXNB - 1, usable_count), extra)
    columns_list = [regs]
    for j in range(1, MAXNB):
        columns_list.append(jnp.where(j <= extra, sorted_options[:, j - 1], regs))
    return (jnp.stack(columns_list, axis=1).astype(jnp.int32), (1 + extra).astype(jnp.int32))


def draw_attended(key, part):
    return list_tables(key)[0]


def draw_counts(key, part):
    return list_tables(key)[1]


def level_of(rng, dims, pieces, low, high):
    level = 1.0
    for axis_at, shards_of in pieces:
        draws = jax.random.uniform(jax.random.fold_in(jax.random.fold_in(rng, 6), axis_at), (shards_of,), jnp.float32, low / len(pieces), high / len(pieces))
        level = level * jnp.repeat(jnp.exp(draws), dims[axis_at] // shards_of).reshape((-1,) + (1,) * (len(dims) - 1 - axis_at))
    return level


def gaussian(stream_key, dims, scale, reach, shards=(), held_as=jnp.bfloat16):
    values = scale * jax.random.normal(stream_key, dims, jnp.float32)
    if shards:
        values = values * level_of(stream_key, dims, shards, -0.22, 0.18)
    return jnp.clip(values, -reach, reach).astype(held_as)


def setup_inputs(seed: int = 0) -> dict:
    arg_keys = jax.random.split(jax.random.key(seed), 8)
    query = draw_query(jax.random.fold_in(arg_keys[7], 71), 0)
    key_in = draw_key_in(jax.random.fold_in(arg_keys[7], 71), 0)
    value = gaussian(arg_keys[2], (SAMPLES, TOKENS, D), 1.0, 6.0, ((0, 4), (1, 64)))
    d_out = gaussian(arg_keys[3], (SAMPLES, TOKENS, D), 1.0, 6.0, ((0, 4), (1, 64)))
    out_weight = gaussian(arg_keys[4], (D, D), D ** -0.5, 0.1875)
    attended = draw_attended(jax.random.fold_in(arg_keys[7], 71), 0)
    counts = draw_counts(jax.random.fold_in(arg_keys[7], 71), 0)
    return dict(query=query, key_in=key_in, value=value, d_out=d_out, out_weight=out_weight, attended=attended, counts=counts)


def reference(query, key_in, value, d_out, out_weight, attended, counts):
    scale = HEAD_DIM ** -0.5

    def one_sample(arrays):
        q_all, k_all, v_all, g_all = arrays

        def step(carry, region):
            key_acc, value_acc, weight_acc = carry
            listed = attended[region]
            slot_valid = jnp.arange(MAXNB) < counts[region]
            starts = (listed * REGION_TOK).astype(jnp.int32)
            keys = jnp.concatenate([lax.dynamic_slice_in_dim(k_all, starts[j], REGION_TOK, 0) for j in range(MAXNB)])
            vals = jnp.concatenate([lax.dynamic_slice_in_dim(v_all, starts[j], REGION_TOK, 0) for j in range(MAXNB)])
            key_valid = jnp.repeat(slot_valid, REGION_TOK)
            begin = (region * REGION_TOK).astype(jnp.int32)
            q_rows = lax.dynamic_slice_in_dim(q_all, begin, REGION_TOK, 0)
            g_rows = lax.dynamic_slice_in_dim(g_all, begin, REGION_TOK, 0)
            q_heads = q_rows.astype(jnp.float32).reshape(REGION_TOK, HEADS, HEAD_DIM)
            k_heads = keys.astype(jnp.float32).reshape(-1, HEADS, HEAD_DIM)
            v_heads = vals.astype(jnp.float32).reshape(-1, HEADS, HEAD_DIM)
            scores = jnp.einsum("thd,khd->htk", q_heads, k_heads) * scale
            scores = jnp.where(key_valid[None, None, :], scores, -1e30)
            largest = jnp.max(scores, axis=-1, keepdims=True)
            weights = jnp.exp(scores - largest)
            probs_f = weights / jnp.sum(weights, axis=-1, keepdims=True)
            probs = probs_f.astype(jnp.bfloat16).astype(jnp.float32)
            attn = jnp.einsum("htk,khd->thd", probs, v_heads).reshape(REGION_TOK, D).astype(jnp.bfloat16)
            layer = jnp.dot(attn, out_weight, preferred_element_type=jnp.float32).astype(jnp.bfloat16)
            d_attn = jnp.dot(g_rows, out_weight.T, preferred_element_type=jnp.float32).astype(jnp.bfloat16)
            weight_acc = weight_acc + jnp.dot(attn.T, g_rows, preferred_element_type=jnp.float32)
            d_heads = d_attn.astype(jnp.float32).reshape(REGION_TOK, HEADS, HEAD_DIM)
            dprob = jnp.einsum("thd,khd->htk", d_heads, v_heads)
            center = jnp.sum(probs_f * dprob, axis=-1, keepdims=True)
            dscore = (probs_f * (dprob - center) * scale).astype(jnp.bfloat16).astype(jnp.float32)
            d_rows = jnp.einsum("htk,khd->thd", dscore, k_heads).reshape(REGION_TOK, D).astype(jnp.bfloat16)
            key_grad = jnp.einsum("htk,thd->khd", dscore, q_heads).reshape(MAXNB, REGION_TOK, D)
            value_grad = jnp.einsum("htk,thd->khd", probs, d_heads).reshape(MAXNB, REGION_TOK, D)
            for j in range(MAXNB):
                old_key = lax.dynamic_slice_in_dim(key_acc, starts[j], REGION_TOK, 0)
                key_acc = lax.dynamic_update_slice_in_dim(key_acc, old_key + key_grad[j], starts[j], 0)
                old_value = lax.dynamic_slice_in_dim(value_acc, starts[j], REGION_TOK, 0)
                value_acc = lax.dynamic_update_slice_in_dim(value_acc, old_value + value_grad[j], starts[j], 0)
            return (key_acc, value_acc, weight_acc), (layer, d_rows)

        start_state = (jnp.zeros((TOKENS, D), jnp.float32), jnp.zeros((TOKENS, D), jnp.float32), jnp.zeros((D, D), jnp.float32))
        final, stacked = lax.scan(step, start_state, jnp.arange(REGIONS, dtype=jnp.int32))
        key_acc, value_acc, weight_acc = final
        layers, d_rows = stacked
        return (layers.reshape(TOKENS, D), d_rows.reshape(TOKENS, D), key_acc.astype(jnp.bfloat16), value_acc.astype(jnp.bfloat16), weight_acc)

    outs = lax.map(one_sample, (query, key_in, value, d_out))
    return outs[0], outs[1], outs[2], outs[3], jnp.sum(outs[4], axis=0)
```

```python
import functools
import jax
import jax.numpy as jnp
from jax import lax
from jax.experimental import pallas as pl
from jax.experimental.pallas import tpu as pltpu
from jax.sharding import PartitionSpec as P

HEAD_DIM = 64
SPAN = 256
F32 = jnp.float32
BF16 = jnp.bfloat16


def nt(a, b):
    return lax.dot_general(a, b, (((1,), (1,)), ((), ())), preferred_element_type=F32)


def tn(a, b):
    return lax.dot_general(a, b, (((0,), (0,)), ((), ())), preferred_element_type=F32)


def nn(a, b):
    return lax.dot_general(a, b, (((1,), (0,)), ((), ())), preferred_element_type=F32)


def half_masks(shape):
    lane = lax.broadcasted_iota(jnp.int32, shape, 1)
    return [lane < HEAD_DIM, lane >= HEAD_DIM]


def local_forward(flags, q, ko, kl, kr, vo, vl, vr, m_out, l_out, o_out):
    seen = [None, flags[0] > 0, flags[1] > 0]
    for g in range(SPAN // 128):
        cols = pl.ds(g * 128, 128)
        queries = q[:, cols] * 0.125
        masks = half_masks(queries.shape)
        keys = [ref[:, cols] for ref in (ko, kl, kr)]
        vals = [ref[:, cols] for ref in (vo, vl, vr)]
        tops, sums, mixes = [], [], []
        for mask in masks:
            part = jnp.where(mask, queries, 0).astype(BF16)
            scores = [nt(part, k) for k in keys]
            scores = [s if f is None else jnp.where(f, s, -1e30) for s, f in zip(scores, seen)]
            top = jnp.max(functools.reduce(jnp.maximum, scores), axis=1, keepdims=True)
            weights = [jnp.exp(s - top) for s in scores]
            sums.append(jnp.sum(weights[0] + weights[1] + weights[2], axis=1, keepdims=True))
            tops.append(top)
            mixes.append(sum(nn(w.astype(BF16), v) for w, v in zip(weights, vals)))
        m_out[:, cols] = jnp.where(masks[0], tops[0], tops[1])
        l_out[:, cols] = jnp.where(masks[0], sums[0], sums[1])
        o_out[:, cols] = jnp.where(masks[0], mixes[0], mixes[1])


def hub_block(flags, q, d, half, rest, m_in, l_in, o_in, attn_out, lse_out, cen_out, dq_out, mine_out, other_out):
    first = flags[2] == 0
    seen = flags[3] > 0
    for g in range(SPAN // 128):
        cols = pl.ds(g * 128, 128)
        queries = q[:, cols] * 0.125
        grads = d[:, cols]
        masks = half_masks(queries.shape)
        a, b = half[:, cols], rest[:, cols]
        key = jnp.where(first, a, b)
        val = jnp.where(first, b, a)
        m_loc, l_loc, o_loc = m_in[:, cols], l_in[:, cols], o_in[:, cols]
        lses, cens, mixes, dqs = [], [], [], []
        dk = dv = 0.0
        for h, mask in enumerate(masks):
            part = jnp.where(mask, queries, 0).astype(BF16)
            gpart = jnp.where(mask, grads, 0).astype(BF16)
            at = slice(h * HEAD_DIM, h * HEAD_DIM + 1)
            scores = jnp.where(seen, nt(part, key), -1e30)
            old = m_loc[:, at]
            top = jnp.maximum(old, jnp.max(scores, axis=1, keepdims=True))
            weights = jnp.exp(scores - top)
            fade = jnp.exp(old - top)
            total = l_loc[:, at] * fade + jnp.sum(weights, axis=1, keepdims=True)
            inv = 1.0 / total
            mix = (o_loc * fade + nn(weights.astype(BF16), val)) * inv
            cen = jnp.sum(jnp.where(mask, mix * grads.astype(F32), 0.0), axis=1, keepdims=True)
            probs = weights * inv
            dscore = (probs * (nt(gpart, val) - cen)).astype(BF16)
            dqs.append(nn(dscore, key))
            dk += tn(dscore, part)
            dv += tn(probs.astype(BF16), gpart)
            lses.append(top + jnp.log(total))
            cens.append(cen)
            mixes.append(mix)
        attn_out[:, cols] = jnp.where(masks[0], mixes[0], mixes[1]).astype(BF16)
        lse_out[:, cols] = jnp.where(masks[0], lses[0], lses[1])
        cen_out[:, cols] = jnp.where(masks[0], cens[0], cens[1])
        dq_out[:, cols] = jnp.where(masks[0], dqs[0], dqs[1])
        mine_out[:, cols] = jnp.where(first, dk, dv).astype(BF16)
        other_out[:, cols] = jnp.where(first, dv, dk).astype(BF16)


def local_backward(flags, q, d, ko, kl, kr, vo, vl, vr, lse_in, cen_in, dq_in, dq_out, own_out, left_out, right_out):
    seen = [None, flags[0] > 0, flags[1] > 0]
    for g in range(SPAN // 128):
        cols = pl.ds(g * 128, 128)
        queries = q[:, cols] * 0.125
        grads = d[:, cols]
        masks = half_masks(queries.shape)
        keys = [ref[:, cols] for ref in (ko, kl, kr)]
        vals = [ref[:, cols] for ref in (vo, vl, vr)]
        lse, cens = lse_in[:, cols], cen_in[:, cols]
        parts = [jnp.where(m, queries, 0).astype(BF16) for m in masks]
        gparts = [jnp.where(m, grads, 0).astype(BF16) for m in masks]
        dq = [0.0, 0.0]
        for key, val, flag, out in zip(keys, vals, seen, (own_out, left_out, right_out)):
            dk = dv = 0.0
            for h in range(2):
                at = slice(h * HEAD_DIM, h * HEAD_DIM + 1)
                scores = nt(parts[h], key)
                if flag is not None:
                    scores = jnp.where(flag, scores, -1e30)
                probs = jnp.exp(scores - lse[:, at])
                dscore = (probs * (nt(gparts[h], val) - cens[:, at])).astype(BF16)
                dq[h] += nn(dscore, key)
                dk += tn(dscore, parts[h])
                dv += tn(probs.astype(BF16), gparts[h])
            out[0, :, cols] = dk.astype(out.dtype)
            out[1, :, cols] = dv.astype(out.dtype)
        total = jnp.where(masks[0], dq[0], dq[1]) + dq_in[:, cols]
        dq_out[:, cols] = (total * 0.125).astype(BF16)


def call(body, ins, outs, flops, name, start=0, count=None):
    width = ins[1].shape[-1]
    steps = width // SPAN if count is None else count

    def spec(shape, shift):
        if len(shape) == 3:
            return pl.BlockSpec((shape[0], shape[1], SPAN), lambda i: (0, 0, i + shift))
        return pl.BlockSpec((shape[0], SPAN), lambda i: (0, i + shift))

    in_specs = [pl.BlockSpec(memory_space=pltpu.SMEM)]
    in_specs += [spec(a.shape, start if a.shape[-1] == width else 0) for a in ins[1:]]
    out_shapes = [jax.ShapeDtypeStruct(tuple(s[:-1]) + (steps * SPAN,), t) for s, t in outs]
    moved = sum(a.size * a.dtype.itemsize for a in ins[1:]) + sum(
        s.size * s.dtype.itemsize for s in out_shapes
    )
    return pl.pallas_call(
        body,
        grid=(steps,),
        in_specs=in_specs,
        out_specs=[spec(s.shape, 0) for s in out_shapes],
        out_shape=out_shapes,
        compiler_params=pltpu.CompilerParams(vmem_limit_bytes=40 * 1024 * 1024),
        cost_estimate=pl.CostEstimate(flops=flops, bytes_accessed=moved, transcendentals=0),
        name=name,
    )(*ins)


NZ, NX, NC = 8, 4, 2


def place(z, x, c):
    return (z % NZ) * NX * NC + (x % NX) * NC + c % NC


def spots():
    return [(z, x, c) for z in range(NZ) for x in range(NX) for c in range(NC)]


def hop(dz=0, dx=0, dc=0):
    return [(place(z, x, c), place(z + dz, x + dx, c + dc)) for z, x, c in spots()]


Z_GROUPS = [[place(z, x, c) for z in range(NZ)] for x in range(NX) for c in range(NC)]


def send(value, pairs):
    return lax.ppermute(value, "region", pairs)


def pick(value, index):
    return lax.dynamic_index_in_dim(value, index, 0, keepdims=False)


def swap_z(value):
    return lax.all_to_all(value, "region", 0, 0, axis_index_groups=Z_GROUPS, tiled=True)


def swap_x(value, x):
    return [pick(value, x)] + [send(pick(value, (x + k) % NX), hop(dx=k)) for k in range(1, NX)]


def gather_x(value, x):
    got = jnp.stack([value] + [send(value, hop(dx=k)) for k in range(1, NX)])
    return jnp.concatenate([pick(got, (x - j) % NX) for j in range(NX)])


def gather_z(value):
    return swap_z(jnp.broadcast_to(value[None], (NZ,) + value.shape))


def shifted(value, step):
    last = NZ * NX * NC
    return send(value, [(i, i + step) for i in range(last) if 0 <= i + step < last])


def on_device(query, key_in, value, d_out, out_weight, attended, counts):
    region = lax.axis_index("region")
    z, x, c = region // (NX * NC), (region // NC) % NX, region % NC
    first = c == 0
    query, key, value, grad_out = query[0], key_in[0], value[0], d_out[0]
    rows, width = query.shape
    listed = attended[0, 1:]
    used = jnp.arange(1, attended.shape[1]) < counts[0]
    left_seen = jnp.any(used & (listed == region - 1))
    right_seen = jnp.any(used & (listed == region + 1))
    far = used & (listed != region - 1) & (listed != region + 1)
    far_local = jnp.max(jnp.where(far, listed, -1))
    flags = jnp.stack([left_seen, right_seen, c, jnp.any(far)]).astype(jnp.int32)

    mine = jnp.where(first, key, value)
    other = jnp.where(first, value, key)
    theirs = send(other, hop(dc=1))
    ids = lax.all_to_all(
        jnp.full((NZ * NX * NC, 1, 128), far_local, jnp.int32), "region", 0, 0, tiled=True
    )
    quarter = rows // NX
    both = jnp.stack(
        [mine.reshape(NX, quarter, width), theirs.reshape(NX, quarter, width)], axis=1
    )
    arrived = jnp.stack(swap_x(both, x))
    hub = jnp.max(ids)
    hub_z, hub_x, hub_c = hub // (NX * NC), (hub // NC) % NX, hub % NC
    picked = pick(arrived, (x - hub_x) % NX)
    piece = jnp.where(hub_c == c, picked[0], picked[1])
    share = pick(swap_z(piece.reshape(NZ, quarter // NZ, width)), hub_z)
    half = gather_x(gather_z(share).reshape(quarter, width), x)
    rest = send(half, hop(dc=1))

    pair = jnp.stack([key, value])
    from_left = shifted(pair, 1)
    from_right = shifted(pair, -1)
    d_attn = lax.dot_general(
        grad_out, out_weight, (((1,), (1,)), ((), ())), preferred_element_type=F32
    ).astype(BF16)

    blocks = [key, from_left[0], from_right[0], value, from_left[1], from_right[1]]
    flat = (rows, width)
    stats = call(
        local_forward, [flags, query, *blocks], [(flat, F32)] * 3, int(1.6e9), "local_forward"
    )
    attn, lse, cen, dq_far, far_mine, far_other = call(
        hub_block,
        [flags, query, d_attn, half, rest, *stats],
        [(flat, BF16), (flat, F32), (flat, F32), (flat, F32), (flat, BF16), (flat, BF16)],
        int(2e9),
        "hub_block",
    )

    summed = (far_mine.astype(F32) + send(far_other, hop(dc=1)).astype(F32)).astype(BF16)
    parts = swap_x(summed.reshape(NX, quarter, width), x)
    summed = sum(p.astype(F32) for p in parts).astype(BF16)
    parts = swap_z(summed.reshape(NZ, quarter // NZ, width))
    total = jnp.sum(parts.astype(F32), axis=0).astype(BF16)
    far_half = gather_x(gather_z(total).reshape(quarter, width), x)
    far_rest = send(far_half, hop(dc=1))

    double = (2,) + flat
    d_query, own, to_left, to_right = call(
        local_backward,
        [flags, query, d_attn, *blocks, lse, cen, dq_far],
        [(flat, BF16), (double, F32), (double, BF16), (double, BF16)],
        int(4e9),
        "local_backward",
    )
    own = own + shifted(to_left, -1).astype(F32) + shifted(to_right, 1).astype(F32)
    at_hub = region == hub
    far_key = jnp.where(first, far_half, far_rest).astype(F32)
    far_value = jnp.where(first, far_rest, far_half).astype(F32)
    d_key = (own[0] + jnp.where(at_hub, far_key, 0.0)).astype(BF16)
    d_value = (own[1] + jnp.where(at_hub, far_value, 0.0)).astype(BF16)

    slab = width // (NZ * NX * NC)
    partial = tn(attn, grad_out).reshape(NZ, NX, NC, slab, width)
    kept = jnp.where(first, partial[:, :, 0], partial[:, :, 1])
    sent = jnp.where(first, partial[:, :, 1], partial[:, :, 0])
    turned = send(sent.astype(BF16), hop(dc=1))
    weight = (kept + turned.astype(F32)).astype(BF16).transpose(1, 0, 2, 3)
    weight = sum(p.astype(F32) for p in swap_x(weight, x)).astype(BF16)
    weight = jnp.sum(swap_z(weight).astype(F32), axis=0)
    dp = lax.axis_size("dp")
    d_weight = weight
    for k in range(1, dp):
        d_weight = d_weight + lax.ppermute(weight, "dp", [(i, (i + k) % dp) for i in range(dp)])

    layer = nn(attn, out_weight).astype(BF16)
    return layer[None], d_query[None], d_key[None], d_value[None], d_weight


def solution(mesh):
    rows = P("dp", "region", None)
    return jax.shard_map(
        on_device,
        mesh=mesh,
        in_specs=(rows, rows, rows, rows, P(), P("region", None), P("region")),
        out_specs=(rows, rows, rows, rows, P("region", None)),
        check_vma=False,
    )
```

```python
import jax
import jax.numpy as jnp
from jax import lax
from jax.experimental import pallas as pl
from jax.experimental.pallas import tpu as pltpu
from jax.sharding import PartitionSpec as P

HEAD_DIM = 64
NZ, NX, NC = 8, 4, 2
SPAN = 256
F32 = jnp.float32
BF16 = jnp.bfloat16
NEVER = -1e30


def nt(a, b):
    return lax.dot_general(a, b, (((1,), (1,)), ((), ())), preferred_element_type=F32)


def tn(a, b):
    return lax.dot_general(a, b, (((0,), (0,)), ((), ())), preferred_element_type=F32)


def nn(a, b):
    return lax.dot_general(a, b, (((1,), (0,)), ((), ())), preferred_element_type=F32)


def half_masks(shape):
    lane = lax.broadcasted_iota(jnp.int32, shape, 1)
    return [lane < HEAD_DIM, lane >= HEAD_DIM]


def local_forward(flags, q, own, left, right, m_out, l_out, o_out):
    seen = [None, flags[0] > 0, flags[1] > 0]
    for g in range(SPAN // 128):
        cols = pl.ds(g * 128, 128)
        queries = q[:, cols] * 0.125
        masks = half_masks(queries.shape)
        keys = [ref[0, :, cols] for ref in (own, left, right)]
        vals = [ref[1, :, cols] for ref in (own, left, right)]
        tops, sums, mixes = [], [], []
        for mask in masks:
            part = jnp.where(mask, queries, 0).astype(BF16)
            scores = [nt(part, k) for k in keys]
            tops_of = [jnp.max(s, axis=1, keepdims=True) for s in scores]
            top = tops_of[0]
            for t, f in zip(tops_of[1:], seen[1:]):
                top = jnp.maximum(top, jnp.where(f, t, NEVER))
            shifts = [top if f is None else jnp.where(f, top, -NEVER) for f in seen]
            weights = [jnp.exp(s - t) for s, t in zip(scores, shifts)]
            sums.append(jnp.sum(weights[0] + weights[1] + weights[2], axis=1, keepdims=True))
            tops.append(top)
            mixes.append(sum(nn(w.astype(BF16), v) for w, v in zip(weights, vals)))
        m_out[:, cols] = jnp.where(masks[0], tops[0], tops[1])
        l_out[:, cols] = jnp.where(masks[0], sums[0], sums[1])
        o_out[:, cols] = jnp.where(masks[0], mixes[0], mixes[1])


def hub_block(
    flags, q, d, half, rest, m_in, l_in, o_in, grad,
    attn_out, lse_out, cen_out, dq_out, mine_out, other_out, kept_out, sent_out,
):
    first = flags[2] == 0
    seen = flags[3] > 0
    for g in range(SPAN // 128):
        cols = pl.ds(g * 128, 128)
        queries = q[:, cols] * 0.125
        grads = d[:, cols]
        masks = half_masks(queries.shape)
        a, b = half[:, cols], rest[:, cols]
        key = jnp.where(first, a, b)
        val = jnp.where(first, b, a)
        m_loc, l_loc, o_loc = m_in[:, cols], l_in[:, cols], o_in[:, cols]
        lses, cens, mixes, dqs = [], [], [], []
        dk = dv = 0.0
        for h, mask in enumerate(masks):
            part = jnp.where(mask, queries, 0).astype(BF16)
            gpart = jnp.where(mask, grads, 0).astype(BF16)
            at = slice(h * HEAD_DIM, h * HEAD_DIM + 1)
            scores = nt(part, key)
            old = m_loc[:, at]
            top = jnp.max(scores, axis=1, keepdims=True)
            top = jnp.maximum(old, jnp.where(seen, top, NEVER))
            weights = jnp.exp(scores - jnp.where(seen, top, -NEVER))
            fade = jnp.exp(old - top)
            total = l_loc[:, at] * fade + jnp.sum(weights, axis=1, keepdims=True)
            inv = 1.0 / total
            coarse = weights.astype(BF16)
            mix = (o_loc * fade + nn(coarse, val)) * inv
            cen = jnp.sum(mix * gpart.astype(F32), axis=1, keepdims=True)
            dscore = (weights * (nt(gpart, val) - cen)).astype(BF16)
            dqs.append(nn(dscore, key) * inv)
            dk += tn(dscore, (part.astype(F32) * inv).astype(BF16))
            dv += tn(coarse, (gpart.astype(F32) * inv).astype(BF16))
            lses.append(top + jnp.log(total))
            cens.append(cen)
            mixes.append(mix)
        attn = jnp.where(masks[0], mixes[0], mixes[1]).astype(BF16)
        attn_out[:, cols] = attn
        weight = tn(attn, grad[...])
        slab = weight.shape[0] // (NX * NC)
        weight = weight.reshape(NX, NC, slab, weight.shape[1])
        for j in range(NX):
            slot = (j - flags[4] + NX) % NX
            kept_out[slot, g] = jnp.where(first, weight[j, 0], weight[j, 1])
            sent_out[slot, g] = jnp.where(first, weight[j, 1], weight[j, 0]).astype(BF16)
        lse_out[:, cols] = jnp.where(masks[0], lses[0], lses[1])
        cen_out[:, cols] = jnp.where(masks[0], cens[0], cens[1])
        dq_out[:, cols] = jnp.where(masks[0], dqs[0], dqs[1])
        mine_out[:, cols] = jnp.where(first, dk, dv).astype(BF16)
        other_out[:, cols] = jnp.where(first, dv, dk).astype(BF16)


def local_backward(flags, q, d, own, left, right, lse_in, cen_in, dq_in, dq_out, own_out, left_out, right_out):
    seen = [None, flags[0] > 0, flags[1] > 0]
    for g in range(SPAN // 128):
        cols = pl.ds(g * 128, 128)
        queries = q[:, cols] * 0.125
        grads = d[:, cols]
        masks = half_masks(queries.shape)
        keys = [ref[0, :, cols] for ref in (own, left, right)]
        vals = [ref[1, :, cols] for ref in (own, left, right)]
        lse, cens = lse_in[:, cols], cen_in[:, cols]
        parts = [jnp.where(m, queries, 0).astype(BF16) for m in masks]
        gparts = [jnp.where(m, grads, 0).astype(BF16) for m in masks]
        dq = [0.0, 0.0]
        for key, val, flag, out in zip(keys, vals, seen, (own_out, left_out, right_out)):
            dk = dv = 0.0
            for h in range(2):
                at = slice(h * HEAD_DIM, h * HEAD_DIM + 1)
                shift = lse[:, at]
                if flag is not None:
                    shift = jnp.where(flag, shift, -NEVER)
                probs = jnp.exp(nt(parts[h], key) - shift)
                dscore = (probs * (nt(gparts[h], val) - cens[:, at])).astype(BF16)
                dq[h] += nn(dscore, key)
                dk += tn(dscore, parts[h])
                dv += tn(probs.astype(BF16), gparts[h])
            out[0, :, cols] = dk.astype(out.dtype)
            out[1, :, cols] = dv.astype(out.dtype)
        total = jnp.where(masks[0], dq[0], dq[1]) + dq_in[:, cols]
        dq_out[:, cols] = (total * 0.125).astype(BF16)


def prepare(spot, listed, counts, key, value, ids_out, flags_out, pair, *pieces):
    region = spot[0]
    left = right = far = jnp.int32(0)
    hub = jnp.int32(-1)
    for j in range(1, listed.shape[1]):
        entry = listed[0, j]
        used = j < counts[0]
        on_left, on_right = entry == region - 1, entry == region + 1
        beside = on_left | on_right
        left = jnp.where(used & on_left, 1, left)
        right = jnp.where(used & on_right, 1, right)
        far = jnp.where(used & jnp.logical_not(beside), 1, far)
        hub = jnp.where(used & jnp.logical_not(beside), entry, hub)
    x = region // NC % NX
    flags_out[0] = left
    flags_out[1] = right
    flags_out[2] = region % NC
    flags_out[3] = far
    flags_out[4] = x
    flags_out[5] = region
    flags_out[6] = 0
    flags_out[7] = 0
    ids_out[...] = jnp.full(ids_out.shape, hub, jnp.int32)
    pair[0] = key[...]
    pair[1] = value[...]
    quarter = pieces[0].shape[1]
    for k, out in enumerate(pieces):
        rows = pl.ds(pl.multiple_of((x + k) % NX * quarter, quarter), quarter)
        out[0] = key[rows, :]
        out[1] = value[rows, :]


def add_pieces(mine, theirs, *pieces):
    for out, k in zip(pieces, range(NX)):
        out[...] = (mine[k].astype(F32) + theirs[k].astype(F32)).astype(BF16)


def simple(body, ins, outs, name, scalars=0):
    smem = pl.BlockSpec(memory_space=pltpu.SMEM)
    vmem = pl.BlockSpec(memory_space=pltpu.VMEM)
    return pl.pallas_call(
        body,
        in_specs=[smem] * scalars + [vmem] * (len(ins) - scalars),
        out_specs=[smem if s == (8,) else vmem for s, _ in outs],
        out_shape=[jax.ShapeDtypeStruct(s, t) for s, t in outs],
        compiler_params=pltpu.CompilerParams(vmem_limit_bytes=32 * 1024 * 1024),
        name=name,
    )(*ins)


def local_backward_into(flags, *refs):
    local_backward(flags, *refs[:8], *refs[9:])


def choose(flags, ids, own, one, two, three, mine_out, other_out, flags_out):
    hub = jnp.max(ids[...])
    c, x = flags[2], flags[4]
    hub_z, hub_x, hub_c = hub // (NX * NC), hub // NC % NX, hub % NC
    for i in range(5):
        flags_out[i] = flags[i]
    flags_out[5] = (hub == flags[5]).astype(jnp.int32)
    flags_out[6] = hub_z
    flags_out[7] = (hub_c == c).astype(jnp.int32)
    for k, ref in enumerate((own, one, two, three)):

        @pl.when((x - hub_x + NX) % NX == k)
        def _():
            mine_out[...] = ref[c]
            other_out[...] = ref[1 - c]


def combine(flags, *refs):
    owns, lefts, rights = refs[0:2], refs[2:4], refs[4:6]
    far_half, far_rest, key_out, value_out = refs[6:]
    first = flags[2] == 0
    at_hub = flags[5] > 0
    tall = key_out.shape[0]
    quarter = far_half.shape[0] // NX
    for j in range(tall // quarter):
        spot = pl.program_id(0) * (tall // quarter) + j
        begin = pl.multiple_of((flags[4] - spot + NX) % NX * quarter, quarter)
        rows = pl.ds(j * quarter, quarter)
        at = 0
        for own, left, right in zip(owns, lefts, rights):
            cols = pl.ds(at, own.shape[-1])
            at += own.shape[-1]
            total = own[:, rows] + left[:, rows].astype(F32) + right[:, rows].astype(F32)
            half = far_half[pl.ds(begin, quarter), cols].astype(F32)
            rest = far_rest[pl.ds(begin, quarter), cols].astype(F32)
            far_key = jnp.where(first, half, rest)
            far_value = jnp.where(first, rest, half)
            key_out[rows, cols] = (total[0] + jnp.where(at_hub, far_key, 0.0)).astype(BF16)
            value_out[rows, cols] = (total[1] + jnp.where(at_hub, far_value, 0.0)).astype(BF16)


def across(shape, start=0):
    lead = (0,) * (len(shape) - 1)
    return pl.BlockSpec(tuple(shape[:-1]) + (SPAN,), lambda i, flags: lead + (i + start,))


def call(body, flags, ins, outs, steps, flops, name, aliases={}):
    shapes = [jax.ShapeDtypeStruct(s, t) for s, t, _ in outs]
    arrays = [a for a, _ in ins]
    moved = sum(a.size * a.dtype.itemsize for a in arrays + shapes)
    return pl.pallas_call(
        body,
        grid_spec=pltpu.PrefetchScalarGridSpec(
            num_scalar_prefetch=1,
            grid=(steps,),
            in_specs=[p or across(a.shape) for a, p in ins],
            out_specs=[p or across(s) for s, _, p in outs],
        ),
        out_shape=shapes,
        compiler_params=pltpu.CompilerParams(vmem_limit_bytes=56 * 1024 * 1024),
        cost_estimate=pl.CostEstimate(flops=flops, bytes_accessed=moved, transcendentals=0),
        input_output_aliases=aliases,
        name=name,
    )(flags, *arrays)


def place(z, x, c):
    return (z % NZ) * NX * NC + (x % NX) * NC + c % NC


def spots():
    return [(z, x, c) for z in range(NZ) for x in range(NX) for c in range(NC)]


def hop(dx=0, dc=0):
    return [(place(z, x, c), place(z, x + dx, c + dc)) for z, x, c in spots()]


Z_GROUPS = [[place(z, x, c) for z in range(NZ)] for x in range(NX) for c in range(NC)]


def send(value, pairs):
    return lax.ppermute(value, "region", pairs)


def pick(value, index):
    return lax.dynamic_index_in_dim(value, index, 0, keepdims=False)


def swap_z(value):
    return lax.all_to_all(value, "region", 0, 0, axis_index_groups=Z_GROUPS, tiled=True)


def gather_z(value):
    out = swap_z(jnp.broadcast_to(value[None], (NZ,) + value.shape))
    return out.reshape((-1,) + value.shape[1:])


def gather_x(value):
    return jnp.concatenate([value] + [send(value, hop(dx=k)) for k in range(1, NX)])


def sum_x(pieces):
    got = [pieces[0]] + [send(pieces[k], hop(dx=k)) for k in range(1, NX)]
    return sum(g.astype(F32) for g in got)


def shifted(value, step):
    last = NZ * NX * NC
    return send(value, [(i, i + step) for i in range(last) if 0 <= i + step < last])


def on_device(query, key_in, value, d_out, out_weight, attended, counts):
    region = lax.axis_index("region")
    x, c = (region // NC) % NX, region % NC
    first = c == 0
    query, key, value, grad_out = query[0], key_in[0], value[0], d_out[0]
    rows, width = query.shape
    quarter, eighth = rows // NX, rows // (NX * NZ)
    spots_count = NZ * NX * NC
    ids, flags, pair, *pieces = simple(
        prepare,
        [jnp.reshape(region, (1,)), attended, counts, key, value],
        [((spots_count, 1, 128), jnp.int32), ((8,), jnp.int32), ((2, rows, width), BF16)]
        + [((2, quarter, width), BF16)] * NX,
        "prepare",
        3,
    )
    arrived = [pieces[0]] + [send(pieces[k], hop(dx=k)) for k in range(1, NX)]
    ids = lax.all_to_all(ids, "region", 0, 0, tiled=True)
    mine, other, flags = simple(
        choose,
        [flags, ids, *arrived],
        [((quarter, width), BF16)] * 2 + [((8,), jnp.int32)],
        "choose",
        1,
    )
    part = jnp.where(flags[7] > 0, mine, send(other, hop(dc=1)))
    part, pair = lax.optimization_barrier((part, pair))
    near = [pair, shifted(pair, 1), shifted(pair, -1)]
    share = pick(swap_z(part.reshape(NZ, eighth, width)), flags[6])
    share, near = lax.optimization_barrier((share, near))

    flat, double = (rows, width), (2, rows, width)
    stats = call(
        local_forward,
        flags,
        [(a, None) for a in (query, *near)],
        [(flat, F32, None)] * 3,
        width // SPAN,
        int(5e9),
        "local_forward",
    )
    d_attn = lax.dot_general(
        grad_out, out_weight, (((1,), (1,)), ((), ())), preferred_element_type=F32
    ).astype(BF16)
    spread, stats, d_attn = lax.optimization_barrier((gather_z(share), stats, d_attn))
    half = gather_x(spread)
    rest = send(half, hop(dc=1))

    slab = width // (NZ * NX * NC)
    by_spot = (NX, NZ, slab, width)
    spot_block = pl.BlockSpec((NX, SPAN // 128, slab, width), lambda i, flags: (0, i, 0, 0))
    whole = pl.BlockSpec(flat, lambda i, flags: (0, 0))
    attn, lse, cen, dq_far, far_mine, far_other, kept, sent = call(
        hub_block,
        flags,
        [(a, None) for a in (query, d_attn, half, rest, *stats)] + [(grad_out, whole)],
        [(flat, t, None) for t in (BF16, F32, F32, F32, BF16, BF16)]
        + [(by_spot, F32, spot_block), (by_spot, BF16, spot_block)],
        width // SPAN,
        int(9e9),
        "hub_block",
    )

    stacked = (NX, quarter, width)
    pieces = simple(
        add_pieces,
        [far_mine.reshape(stacked), send(far_other, hop(dc=1)).reshape(stacked)],
        [((quarter, width), BF16)] * NX,
        "add_pieces",
    )
    pieces = [pieces[-k % NX] for k in range(NX)]
    turned = send(sent, hop(dc=1))
    pieces, kept, attn = lax.optimization_barrier((pieces, kept, attn))
    slabs = simple(add_pieces, [kept, turned], [((NZ, slab, width), BF16)] * NX, "add_slabs")
    layer = nn(attn, out_weight).astype(BF16)
    pieces = [pieces[0]] + [send(pieces[k], hop(dx=k)) for k in range(1, NX)]
    pieces, slabs, layer, lse = lax.optimization_barrier((pieces, slabs, layer, lse))
    summed = sum(p.astype(F32) for p in pieces).astype(BF16)

    def backward(lse, d_query, begin, steps):
        inputs = (query, d_attn, *near, lse, cen, dq_far)
        ins = [(a, across(a.shape, begin)) for a in inputs]
        wide = (2, rows, steps * SPAN)
        body, aliases = local_backward, {}
        if d_query is not None:
            body, aliases = local_backward_into, {1 + len(ins): 0}
            ins = ins + [(d_query, pl.BlockSpec(memory_space=pl.ANY))]
        return call(
            body,
            flags,
            ins,
            [(flat, BF16, across(flat, begin))]
            + [(wide, F32, None), (wide, BF16, None), (wide, BF16, None)],
            steps,
            int(2e9) * steps,
            "local_backward",
            aliases,
        )

    d_query, *first_part = backward(lse, None, 0, 2)
    slabs = [slabs[0]] + [send(slabs[k], hop(dx=k)) for k in range(1, NX)]
    summed, first_part, lse = lax.optimization_barrier(
        (swap_z(summed.reshape(NZ, eighth, width)), first_part, lse)
    )
    total = jnp.sum(summed.astype(F32), axis=0).astype(BF16)
    weight = sum(p.astype(F32) for p in slabs).astype(BF16)
    sides = [shifted(first_part[1], -1), shifted(first_part[2], 1)]
    d_query, *second_part = backward(lse, d_query, 2, 2)
    both = jnp.concatenate([jnp.broadcast_to(total[None], (NZ,) + total.shape), weight], axis=1)
    both, second_part, sides = lax.optimization_barrier((swap_z(both), second_part, sides))
    far_half = gather_x(both[:, :eighth].reshape(quarter, width))
    weight, far_half = lax.optimization_barrier((both[:, eighth:], far_half))
    far_rest = send(far_half, hop(dc=1))
    weight = jnp.sum(weight.astype(F32), axis=0)
    parts = [first_part, second_part]
    rights = [sides[0], shifted(second_part[1], -1)]
    lefts = [sides[1], shifted(second_part[2], 1)]
    dp = lax.axis_size("dp")
    shares = [
        lax.ppermute(weight, "dp", [(i, (i + k) % dp) for i in range(dp)]) for k in range(1, dp)
    ]

    tall = rows // 2

    def pair_block(a):
        return pl.BlockSpec((2, tall, a.shape[-1]), lambda i, flags: (0, i, 0))

    d_key, d_value = call(
        combine,
        flags,
        [(a, pair_block(a)) for a in (*[p[0] for p in parts], *lefts, *rights)]
        + [(a, whole) for a in (far_half, far_rest)],
        [(flat, BF16, pl.BlockSpec((tall, width), lambda i, flags: (i, 0)))] * 2,
        2,
        int(1e6),
        "combine",
    )
    d_key, shares = lax.optimization_barrier((d_key, shares))
    d_weight = weight + sum(shares)
    return layer[None], d_query[None], d_key[None], d_value[None], d_weight


def solution(mesh):
    rows = P("dp", "region", None)
    return jax.shard_map(
        on_device,
        mesh=mesh,
        in_specs=(rows, rows, rows, rows, P(), P("region", None), P("region")),
        out_specs=(rows, rows, rows, rows, P("region", None)),
        check_vma=False,
    )
```

```python
import jax
import jax.numpy as jnp
from jax import lax
from jax.experimental import pallas as pl
from jax.experimental.pallas import tpu as pltpu
from jax.sharding import PartitionSpec as P

HEAD_DIM = 64
NZ, NX, NC = 8, 4, 2
SPAN = 256
F32 = jnp.float32
BF16 = jnp.bfloat16
NEVER = -1e30


def nt(a, b):
    return lax.dot_general(a, b, (((1,), (1,)), ((), ())), preferred_element_type=F32)


def tn(a, b):
    return lax.dot_general(a, b, (((0,), (0,)), ((), ())), preferred_element_type=F32)


def nn(a, b):
    return lax.dot_general(a, b, (((1,), (0,)), ((), ())), preferred_element_type=F32)


def half_masks(shape):
    lane = lax.broadcasted_iota(jnp.int32, shape, 1)
    return [lane < HEAD_DIM, lane >= HEAD_DIM]


def local_forward(flags, q, own, core, chip, m_out, l_out, o_out):
    seen = [None, flags[0] > 0, flags[1] > 0]
    for g in range(SPAN // 128):
        cols = pl.ds(g * 128, 128)
        queries = q[:, cols] * 0.125
        masks = half_masks(queries.shape)
        keys = [ref[0, :, cols] for ref in (own, core, chip)]
        vals = [ref[1, :, cols] for ref in (own, core, chip)]
        tops, sums, mixes = [], [], []
        for mask in masks:
            part = jnp.where(mask, queries, 0).astype(BF16)
            scores = [nt(part, k) for k in keys]
            tops_of = [jnp.max(s, axis=1, keepdims=True) for s in scores]
            top = tops_of[0]
            for t, f in zip(tops_of[1:], seen[1:]):
                top = jnp.maximum(top, jnp.where(f, t, NEVER))
            shifts = [top if f is None else jnp.where(f, top, -NEVER) for f in seen]
            weights = [jnp.exp(s - t) for s, t in zip(scores, shifts)]
            sums.append(jnp.sum(weights[0] + weights[1] + weights[2], axis=1, keepdims=True))
            tops.append(top)
            mixes.append(sum(nn(w.astype(BF16), v) for w, v in zip(weights, vals)))
        m_out[:, cols] = jnp.where(masks[0], tops[0], tops[1])
        l_out[:, cols] = jnp.where(masks[0], sums[0], sums[1])
        o_out[:, cols] = jnp.where(masks[0], mixes[0], mixes[1])


def hub_block(
    flags, q, d, half, rest, m_in, l_in, o_in, grad,
    attn_out, lse_out, cen_out, dq_out, mine_out, other_out, kept_out, sent_out,
):
    first = flags[2] == 0
    seen = flags[3] > 0
    for g in range(SPAN // 128):
        cols = pl.ds(g * 128, 128)
        queries = q[:, cols] * 0.125
        grads = d[:, cols]
        masks = half_masks(queries.shape)
        a, b = half[:, cols], rest[:, cols]
        key = jnp.where(first, a, b)
        val = jnp.where(first, b, a)
        m_loc, l_loc, o_loc = m_in[:, cols], l_in[:, cols], o_in[:, cols]
        lses, cens, mixes, dqs = [], [], [], []
        dk = dv = 0.0
        for h, mask in enumerate(masks):
            part = jnp.where(mask, queries, 0).astype(BF16)
            gpart = jnp.where(mask, grads, 0).astype(BF16)
            at = slice(h * HEAD_DIM, h * HEAD_DIM + 1)
            scores = nt(part, key)
            old = m_loc[:, at]
            top = jnp.max(scores, axis=1, keepdims=True)
            top = jnp.maximum(old, jnp.where(seen, top, NEVER))
            weights = jnp.exp(scores - jnp.where(seen, top, -NEVER))
            fade = jnp.exp(old - top)
            total = l_loc[:, at] * fade + jnp.sum(weights, axis=1, keepdims=True)
            inv = 1.0 / total
            coarse = weights.astype(BF16)
            mix = (o_loc * fade + nn(coarse, val)) * inv
            cen = jnp.sum(mix * gpart.astype(F32), axis=1, keepdims=True)
            dscore = (weights * (nt(gpart, val) - cen)).astype(BF16)
            dqs.append(nn(dscore, key) * inv)
            dk += tn(dscore, (part.astype(F32) * inv).astype(BF16))
            dv += tn(coarse, (gpart.astype(F32) * inv).astype(BF16))
            lses.append(top + jnp.log(total))
            cens.append(cen)
            mixes.append(mix)
        attn = jnp.where(masks[0], mixes[0], mixes[1]).astype(BF16)
        attn_out[:, cols] = attn
        weight = tn(attn, grad[...])
        slab = weight.shape[0] // (NX * NC)
        weight = weight.reshape(NX, NC, slab, weight.shape[1])
        for j in range(NX):
            slot = (j - flags[4] + NX) % NX
            kept_out[slot, g] = jnp.where(first, weight[j, 0], weight[j, 1])
            sent_out[slot, g] = jnp.where(first, weight[j, 1], weight[j, 0]).astype(BF16)
        lse_out[:, cols] = jnp.where(masks[0], lses[0], lses[1])
        cen_out[:, cols] = jnp.where(masks[0], cens[0], cens[1])
        dq_out[:, cols] = jnp.where(masks[0], dqs[0], dqs[1])
        mine_out[:, cols] = jnp.where(first, dk, dv).astype(BF16)
        other_out[:, cols] = jnp.where(first, dv, dk).astype(BF16)


def local_backward(
    flags, q, d, own, core, chip, lse_in, cen_in, dq_in, dq_out, own_out, core_out, chip_out
):
    seen = [None, flags[0] > 0, flags[1] > 0]
    for g in range(SPAN // 128):
        cols = pl.ds(g * 128, 128)
        queries = q[:, cols] * 0.125
        grads = d[:, cols]
        masks = half_masks(queries.shape)
        keys = [ref[0, :, cols] for ref in (own, core, chip)]
        vals = [ref[1, :, cols] for ref in (own, core, chip)]
        lse, cens = lse_in[:, cols], cen_in[:, cols]
        parts = [jnp.where(m, queries, 0).astype(BF16) for m in masks]
        gparts = [jnp.where(m, grads, 0).astype(BF16) for m in masks]
        dq = [0.0, 0.0]
        for key, val, flag, out in zip(keys, vals, seen, (own_out, core_out, chip_out)):
            dk = dv = 0.0
            for h in range(2):
                at = slice(h * HEAD_DIM, h * HEAD_DIM + 1)
                shift = lse[:, at]
                if flag is not None:
                    shift = jnp.where(flag, shift, -NEVER)
                probs = jnp.exp(nt(parts[h], key) - shift)
                dscore = (probs * (nt(gparts[h], val) - cens[:, at])).astype(BF16)
                dq[h] += nn(dscore, key)
                dk += tn(dscore, parts[h])
                dv += tn(probs.astype(BF16), gparts[h])
            out[0, :, cols] = dk.astype(out.dtype)
            out[1, :, cols] = dv.astype(out.dtype)
        total = jnp.where(masks[0], dq[0], dq[1]) + dq_in[:, cols]
        dq_out[:, cols] = (total * 0.125).astype(BF16)


def prepare(spot, listed, counts, key, value, ids_out, flags_out, pair, *pieces):
    region = spot[0]
    left = right = far = jnp.int32(0)
    hub = jnp.int32(-1)
    for j in range(1, listed.shape[1]):
        entry = listed[0, j]
        used = j < counts[0]
        on_left, on_right = entry == region - 1, entry == region + 1
        beside = on_left | on_right
        left = jnp.where(used & on_left, 1, left)
        right = jnp.where(used & on_right, 1, right)
        far = jnp.where(used & jnp.logical_not(beside), 1, far)
        hub = jnp.where(used & jnp.logical_not(beside), entry, hub)
    x = region // NC % NX
    lower = region % NC == 0
    flags_out[0] = jnp.where(lower, right, left)
    flags_out[1] = jnp.where(lower, left, right)
    flags_out[2] = region % NC
    flags_out[3] = far
    flags_out[4] = x
    flags_out[5] = region
    flags_out[6] = 0
    flags_out[7] = 0
    ids_out[...] = jnp.full(ids_out.shape, hub, jnp.int32)
    pair[0] = key[...]
    pair[1] = value[...]
    quarter = pieces[0].shape[1]
    for k, out in enumerate(pieces):
        rows = pl.ds(pl.multiple_of((x + k) % NX * quarter, quarter), quarter)
        out[0] = key[rows, :]
        out[1] = value[rows, :]


def add_pieces(flags, mine, theirs, kept, turned, *pieces):
    quarter = mine.shape[1]
    for k, out in enumerate(pieces):
        spot = (flags[4] + k) % NX
        far = mine[spot].astype(F32) + theirs[spot].astype(F32)
        out[pl.ds(0, quarter), :] = far.astype(BF16)
        slab = kept[k] + turned[k].astype(F32)
        slab = slab.reshape(-1, slab.shape[-1]).astype(BF16)
        out[pl.ds(quarter, slab.shape[0]), :] = slab


def simple(body, ins, outs, name, scalars=0):
    smem = pl.BlockSpec(memory_space=pltpu.SMEM)
    vmem = pl.BlockSpec(memory_space=pltpu.VMEM)
    return pl.pallas_call(
        body,
        in_specs=[smem] * scalars + [vmem] * (len(ins) - scalars),
        out_specs=[smem if s == (8,) else vmem for s, _ in outs],
        out_shape=[jax.ShapeDtypeStruct(s, t) for s, t in outs],
        compiler_params=pltpu.CompilerParams(vmem_limit_bytes=32 * 1024 * 1024),
        name=name,
    )(*ins)


def local_backward_into(flags, *refs):
    local_backward(flags, *refs[:8], *refs[12:])


def choose(flags, ids, own, one, two, three, mine_out, other_out, flags_out):
    hub = jnp.max(ids[...])
    c, x = flags[2], flags[4]
    hub_z, hub_x, hub_c = hub // (NX * NC), hub // NC % NX, hub % NC
    for i in range(5):
        flags_out[i] = flags[i]
    flags_out[5] = (hub == flags[5]).astype(jnp.int32)
    flags_out[6] = hub_z
    flags_out[7] = (hub_c == c).astype(jnp.int32)
    for k, ref in enumerate((own, one, two, three)):

        @pl.when((x - hub_x + NX) % NX == k)
        def _():
            mine_out[...] = ref[c]
            other_out[...] = ref[1 - c]


def combine(flags, own, from_core, from_chip, far_half, far_rest, key_out, value_out):
    first = flags[2] == 0
    at_hub = flags[5] > 0
    tall = 64
    for begin in range(0, key_out.shape[0], tall):
        rows = pl.ds(begin, tall)
        total = own[:, rows] + from_core[:, rows].astype(F32) + from_chip[:, rows].astype(F32)
        half, rest = far_half[rows, :].astype(F32), far_rest[rows, :].astype(F32)
        far_key = jnp.where(first, half, rest)
        far_value = jnp.where(first, rest, half)
        key_out[rows, :] = (total[0] + jnp.where(at_hub, far_key, 0.0)).astype(BF16)
        value_out[rows, :] = (total[1] + jnp.where(at_hub, far_value, 0.0)).astype(BF16)


def across(shape, start=0):
    lead = (0,) * (len(shape) - 1)
    return pl.BlockSpec(tuple(shape[:-1]) + (SPAN,), lambda i, flags: lead + (i + start,))


def call(body, flags, ins, outs, steps, flops, name, aliases={}):
    shapes = [jax.ShapeDtypeStruct(s, t) for s, t, _ in outs]
    arrays = [a for a, _ in ins]
    moved = sum(a.size * a.dtype.itemsize for a in arrays + shapes)
    return pl.pallas_call(
        body,
        grid_spec=pltpu.PrefetchScalarGridSpec(
            num_scalar_prefetch=1,
            grid=(steps,),
            in_specs=[p or across(a.shape) for a, p in ins],
            out_specs=[p or across(s) for s, _, p in outs],
        ),
        out_shape=shapes,
        compiler_params=pltpu.CompilerParams(vmem_limit_bytes=56 * 1024 * 1024),
        cost_estimate=pl.CostEstimate(flops=flops, bytes_accessed=moved, transcendentals=0),
        input_output_aliases=aliases,
        name=name,
    )(flags, *arrays)


def place(z, x, c):
    return (z % NZ) * NX * NC + (x % NX) * NC + c % NC


def spots():
    return [(z, x, c) for z in range(NZ) for x in range(NX) for c in range(NC)]


def hop(dx=0, dc=0):
    return [(place(z, x, c), place(z, x + dx, c + dc)) for z, x, c in spots()]


Z_GROUPS = [[place(z, x, c) for z in range(NZ)] for x in range(NX) for c in range(NC)]


def send(value, pairs):
    return lax.ppermute(value, "region", pairs)


def pick(value, index):
    return lax.dynamic_index_in_dim(value, index, 0, keepdims=False)


def swap_z(value):
    return lax.all_to_all(value, "region", 0, 0, axis_index_groups=Z_GROUPS, tiled=True)


PLANE_GROUPS = [[place(z, x, c) for x in range(NX) for z in range(NZ)] for c in range(NC)]


def gather_plane(value):
    count = NZ * NX
    out = lax.all_to_all(
        jnp.broadcast_to(value[None], (count,) + value.shape),
        "region",
        0,
        0,
        axis_index_groups=PLANE_GROUPS,
        tiled=True,
    )
    return out.reshape((-1,) + value.shape[1:])


CORE = hop(dc=1)
CHIP = [p for r in range(1, NZ * NX * NC - 1, NC) for p in ((r, r + 1), (r + 1, r))]


def on_device(query, key_in, value, d_out, out_weight, attended, counts):
    region = lax.axis_index("region")
    x, c = (region // NC) % NX, region % NC
    first = c == 0
    query, key, value, grad_out = query[0], key_in[0], value[0], d_out[0]
    rows, width = query.shape
    quarter, eighth = rows // NX, rows // (NX * NZ)
    spots_count = NZ * NX * NC
    ids, flags, pair, *pieces = simple(
        prepare,
        [jnp.reshape(region, (1,)), attended, counts, key, value],
        [((spots_count, 1, 128), jnp.int32), ((8,), jnp.int32), ((2, rows, width), BF16)]
        + [((2, quarter, width), BF16)] * NX,
        "prepare",
        3,
    )
    arrived = [pieces[0]] + [send(pieces[k], hop(dx=k)) for k in range(1, NX)]
    ids = lax.all_to_all(ids, "region", 0, 0, tiled=True)
    mine, other, flags = simple(
        choose,
        [flags, ids, *arrived],
        [((quarter, width), BF16)] * 2 + [((8,), jnp.int32)],
        "choose",
        1,
    )
    part = jnp.where(flags[7] > 0, mine, send(other, hop(dc=1)))
    part, pair = lax.optimization_barrier((part, pair))
    near = [pair, send(pair, CORE), send(pair, CHIP)]
    share = pick(swap_z(part.reshape(NZ, eighth, width)), flags[6])
    share, near = lax.optimization_barrier((share, near))

    flat, double = (rows, width), (2, rows, width)
    stats = call(
        local_forward,
        flags,
        [(a, None) for a in (query, *near)],
        [(flat, F32, None)] * 3,
        width // SPAN,
        int(5e9),
        "local_forward",
    )
    d_attn = lax.dot_general(
        grad_out, out_weight, (((1,), (1,)), ((), ())), preferred_element_type=F32
    ).astype(BF16)
    half, stats, d_attn = lax.optimization_barrier((gather_plane(share), stats, d_attn))
    rest = send(half, hop(dc=1))

    slab = width // (NZ * NX * NC)
    by_spot = (NX, NZ, slab, width)
    spot_block = pl.BlockSpec((NX, SPAN // 128, slab, width), lambda i, flags: (0, i, 0, 0))
    whole = pl.BlockSpec(flat, lambda i, flags: (0, 0))
    attn, lse, cen, dq_far, far_mine, far_other, kept, sent = call(
        hub_block,
        flags,
        [(a, None) for a in (query, d_attn, half, rest, *stats)] + [(grad_out, whole)],
        [(flat, t, None) for t in (BF16, F32, F32, F32, BF16, BF16)]
        + [(by_spot, F32, spot_block), (by_spot, BF16, spot_block)],
        width // SPAN,
        int(9e9),
        "hub_block",
    )

    received = send(far_other, CORE)
    turned = send(sent, CORE)
    layer = nn(attn, out_weight).astype(BF16)
    received, turned, layer = lax.optimization_barrier((received, turned, layer))
    stacked = (NX, quarter, width)
    pieces = simple(
        add_pieces,
        [flags, far_mine.reshape(stacked), received.reshape(stacked), kept, turned],
        [((quarter + NZ * slab, width), BF16)] * NX,
        "add_pieces",
        1,
    )
    pieces, lse = lax.optimization_barrier((pieces, lse))
    pieces = [pieces[0]] + [send(pieces[k], hop(dx=k)) for k in range(1, NX)]

    steps = width // SPAN // 2
    double = (2, rows, width)

    def backward(lse, done, begin):
        ins = [(a, across(a.shape, begin)) for a in (query, d_attn, *near, lse, cen, dq_far)]
        outs = [(flat, BF16), (double, F32), (double, BF16), (double, BF16)]
        return call(
            local_backward_into if done else local_backward,
            flags,
            ins + [(a, pl.BlockSpec(memory_space=pl.ANY)) for a in done],
            [(s, t, across(s, begin)) for s, t in outs],
            steps,
            int(4e9),
            "local_backward",
            {1 + len(ins) + i: i for i in range(len(done))},
        )

    grads = backward(lse, [], 0)
    pieces, grads, lse = lax.optimization_barrier((pieces, grads, lse))
    summed = sum(p.astype(F32) for p in pieces).astype(BF16)
    both = [summed[:quarter].reshape(NZ, eighth, width), summed[quarter:].reshape(NZ, slab, width)]
    both = swap_z(jnp.concatenate(both, axis=1))
    grads = backward(lse, grads, steps)
    both, grads = lax.optimization_barrier((both, grads))
    d_query, own, to_core, to_chip = grads
    total = jnp.sum(both[:, :eighth].astype(F32), axis=0).astype(BF16)
    weight = jnp.sum(both[:, eighth:].astype(F32), axis=0)

    far_half = gather_plane(total)
    from_chip = send(to_chip, CHIP)
    from_core = send(to_core, CORE)
    dp = lax.axis_size("dp")
    shares = [
        lax.ppermute(weight, "dp", [(i, (i + k) % dp) for i in range(dp)]) for k in range(1, dp)
    ]
    far_half, shares, from_chip = lax.optimization_barrier((far_half, shares, from_chip))
    d_weight = weight + sum(shares)
    far_rest = send(far_half, CORE)
    d_key, d_value = simple(
        combine,
        [flags, own, from_core, from_chip, far_half, far_rest],
        [(flat, BF16)] * 2,
        "combine",
        1,
    )
    return layer[None], d_query[None], d_key[None], d_value[None], d_weight


def solution(mesh):
    rows = P("dp", "region", None)
    return jax.shard_map(
        on_device,
        mesh=mesh,
        in_specs=(rows, rows, rows, rows, P(), P("region", None), P("region")),
        out_specs=(rows, rows, rows, rows, P("region", None)),
        check_vma=False,
    )
```

```python
import jax
import jax.numpy as jnp
from jax import lax
from jax.experimental import pallas as pl
from jax.experimental.pallas import tpu as pltpu
from jax.sharding import PartitionSpec as P

HEAD_DIM = 64
NZ, NX, NC = 8, 4, 2
SPAN = 256
F32 = jnp.float32
BF16 = jnp.bfloat16
NEVER = -1e30


def nt(a, b):
    return lax.dot_general(a, b, (((1,), (1,)), ((), ())), preferred_element_type=F32)


def tn(a, b):
    return lax.dot_general(a, b, (((0,), (0,)), ((), ())), preferred_element_type=F32)


def nn(a, b):
    return lax.dot_general(a, b, (((1,), (0,)), ((), ())), preferred_element_type=F32)


def half_masks(shape):
    lane = lax.broadcasted_iota(jnp.int32, shape, 1)
    return [lane < HEAD_DIM, lane >= HEAD_DIM]


def local_forward(flags, q, own, core, chip, m_out, l_out, o_out):
    seen = [None, flags[0] > 0, flags[1] > 0]
    for g in range(SPAN // 128):
        cols = pl.ds(g * 128, 128)
        queries = q[:, cols] * 0.125
        masks = half_masks(queries.shape)
        keys = [ref[0, :, cols] for ref in (own, core, chip)]
        vals = [ref[1, :, cols] for ref in (own, core, chip)]
        tops, sums, mixes = [], [], []
        for mask in masks:
            part = jnp.where(mask, queries, 0).astype(BF16)
            scores = [nt(part, k) for k in keys]
            tops_of = [jnp.max(s, axis=1, keepdims=True) for s in scores]
            top = tops_of[0]
            for t, f in zip(tops_of[1:], seen[1:]):
                top = jnp.maximum(top, jnp.where(f, t, NEVER))
            shifts = [top if f is None else jnp.where(f, top, -NEVER) for f in seen]
            weights = [jnp.exp(s - t) for s, t in zip(scores, shifts)]
            sums.append(jnp.sum(weights[0] + weights[1] + weights[2], axis=1, keepdims=True))
            tops.append(top)
            mixes.append(sum(nn(w.astype(BF16), v) for w, v in zip(weights, vals)))
        m_out[:, cols] = jnp.where(masks[0], tops[0], tops[1])
        l_out[:, cols] = jnp.where(masks[0], sums[0], sums[1])
        o_out[:, cols] = jnp.where(masks[0], mixes[0], mixes[1])


def hub_block(
    flags, q, d, half, rest, m_in, l_in, o_in, grad,
    attn_out, lse_out, cen_out, dq_out, mine_out, other_out, kept_out, sent_out,
):
    first = flags[2] == 0
    seen = flags[3] > 0
    for g in range(SPAN // 128):
        cols = pl.ds(g * 128, 128)
        queries = q[:, cols] * 0.125
        grads = d[:, cols]
        masks = half_masks(queries.shape)
        a, b = half[:, cols], rest[:, cols]
        key = jnp.where(first, a, b)
        val = jnp.where(first, b, a)
        m_loc, l_loc, o_loc = m_in[:, cols], l_in[:, cols], o_in[:, cols]
        lses, cens, mixes, dqs = [], [], [], []
        dk = dv = 0.0
        for h, mask in enumerate(masks):
            part = jnp.where(mask, queries, 0).astype(BF16)
            gpart = jnp.where(mask, grads, 0).astype(BF16)
            at = slice(h * HEAD_DIM, h * HEAD_DIM + 1)
            scores = nt(part, key)
            old = m_loc[:, at]
            top = jnp.max(scores, axis=1, keepdims=True)
            top = jnp.maximum(old, jnp.where(seen, top, NEVER))
            weights = jnp.exp(scores - jnp.where(seen, top, -NEVER))
            fade = jnp.exp(old - top)
            total = l_loc[:, at] * fade + jnp.sum(weights, axis=1, keepdims=True)
            inv = 1.0 / total
            coarse = weights.astype(BF16)
            mix = (o_loc * fade + nn(coarse, val)) * inv
            cen = jnp.sum(mix * gpart.astype(F32), axis=1, keepdims=True)
            dscore = (weights * (nt(gpart, val) - cen)).astype(BF16)
            dqs.append(nn(dscore, key) * inv)
            dk += tn(dscore, (part.astype(F32) * inv).astype(BF16))
            dv += tn(coarse, (gpart.astype(F32) * inv).astype(BF16))
            lses.append(top + jnp.log(total))
            cens.append(cen)
            mixes.append(mix)
        attn = jnp.where(masks[0], mixes[0], mixes[1]).astype(BF16)
        attn_out[:, cols] = attn
        weight = tn(attn, grad[...])
        slab = weight.shape[0] // (NX * NC)
        weight = weight.reshape(NX, NC, slab, weight.shape[1])
        for j in range(NX):
            slot = (j - flags[4] + NX) % NX
            kept_out[slot, g] = jnp.where(first, weight[j, 0], weight[j, 1])
            sent_out[slot, g] = jnp.where(first, weight[j, 1], weight[j, 0]).astype(BF16)
        lse_out[:, cols] = jnp.where(masks[0], lses[0], lses[1])
        cen_out[:, cols] = jnp.where(masks[0], cens[0], cens[1])
        dq_out[:, cols] = jnp.where(masks[0], dqs[0], dqs[1])
        mine_out[:, cols] = jnp.where(first, dk, dv).astype(BF16)
        other_out[:, cols] = jnp.where(first, dv, dk).astype(BF16)


def local_backward(
    flags, q, d, own, core, chip, lse_in, cen_in, dq_in, dq_out, own_out, core_out, chip_out
):
    seen = [None, flags[0] > 0, flags[1] > 0]
    for g in range(SPAN // 128):
        cols = pl.ds(g * 128, 128)
        queries = q[:, cols] * 0.125
        grads = d[:, cols]
        masks = half_masks(queries.shape)
        keys = [ref[0, :, cols] for ref in (own, core, chip)]
        vals = [ref[1, :, cols] for ref in (own, core, chip)]
        lse, cens = lse_in[:, cols], cen_in[:, cols]
        parts = [jnp.where(m, queries, 0).astype(BF16) for m in masks]
        gparts = [jnp.where(m, grads, 0).astype(BF16) for m in masks]
        dq = [0.0, 0.0]
        for key, val, flag, out in zip(keys, vals, seen, (own_out, core_out, chip_out)):
            dk = dv = 0.0
            for h in range(2):
                at = slice(h * HEAD_DIM, h * HEAD_DIM + 1)
                shift = lse[:, at]
                if flag is not None:
                    shift = jnp.where(flag, shift, -NEVER)
                probs = jnp.exp(nt(parts[h], key) - shift)
                dscore = (probs * (nt(gparts[h], val) - cens[:, at])).astype(BF16)
                dq[h] += nn(dscore, key)
                dk += tn(dscore, parts[h])
                dv += tn(probs.astype(BF16), gparts[h])
            out[0, :, cols] = dk.astype(out.dtype)
            out[1, :, cols] = dv.astype(out.dtype)
        total = jnp.where(masks[0], dq[0], dq[1]) + dq_in[:, cols]
        dq_out[:, cols] = (total * 0.125).astype(BF16)


def prepare(spot, listed, counts, key, value, ids_out, flags_out, pair, *pieces):
    region = spot[0]
    left = right = far = jnp.int32(0)
    hub = jnp.int32(-1)
    for j in range(1, listed.shape[1]):
        entry = listed[0, j]
        used = j < counts[0]
        on_left, on_right = entry == region - 1, entry == region + 1
        beside = on_left | on_right
        left = jnp.where(used & on_left, 1, left)
        right = jnp.where(used & on_right, 1, right)
        far = jnp.where(used & jnp.logical_not(beside), 1, far)
        hub = jnp.where(used & jnp.logical_not(beside), entry, hub)
    x = region // NC % NX
    lower = region % NC == 0
    flags_out[0] = jnp.where(lower, right, left)
    flags_out[1] = jnp.where(lower, left, right)
    flags_out[2] = region % NC
    flags_out[3] = far
    flags_out[4] = x
    flags_out[5] = region
    flags_out[6] = 0
    flags_out[7] = 0
    ids_out[...] = jnp.full(ids_out.shape, hub, jnp.int32)
    pair[0] = key[...]
    pair[1] = value[...]
    quarter = pieces[0].shape[1]
    for k, out in enumerate(pieces):
        rows = pl.ds(pl.multiple_of((x + k) % NX * quarter, quarter), quarter)
        out[0] = key[rows, :]
        out[1] = value[rows, :]


def add_pieces(flags, mine, theirs, kept, turned, *pieces):
    quarter = mine.shape[1]
    for k, out in enumerate(pieces):
        spot = (flags[4] + k) % NX
        far = mine[spot].astype(F32) + theirs[spot].astype(F32)
        out[pl.ds(0, quarter), :] = far.astype(BF16)
        slab = kept[k] + turned[k].astype(F32)
        slab = slab.reshape(-1, slab.shape[-1]).astype(BF16)
        out[pl.ds(quarter, slab.shape[0]), :] = slab


def simple(body, ins, outs, name, scalars=0):
    smem = pl.BlockSpec(memory_space=pltpu.SMEM)
    vmem = pl.BlockSpec(memory_space=pltpu.VMEM)
    return pl.pallas_call(
        body,
        in_specs=[smem] * scalars + [vmem] * (len(ins) - scalars),
        out_specs=[smem if s == (8,) else vmem for s, _ in outs],
        out_shape=[jax.ShapeDtypeStruct(s, t) for s, t in outs],
        compiler_params=pltpu.CompilerParams(vmem_limit_bytes=32 * 1024 * 1024),
        name=name,
    )(*ins)


def local_backward_into(flags, *refs):
    local_backward(flags, *refs[:8], *refs[12:])


def choose(flags, ids, own, one, two, three, mine_out, other_out, flags_out):
    hub = jnp.max(ids[...])
    c, x = flags[2], flags[4]
    hub_z, hub_x, hub_c = hub // (NX * NC), hub // NC % NX, hub % NC
    for i in range(5):
        flags_out[i] = flags[i]
    flags_out[5] = (hub == flags[5]).astype(jnp.int32)
    flags_out[6] = hub_z
    flags_out[7] = (hub_c == c).astype(jnp.int32)
    for k, ref in enumerate((own, one, two, three)):

        @pl.when((x - hub_x + NX) % NX == k)
        def _():
            mine_out[...] = ref[c]
            other_out[...] = ref[1 - c]


def combine(flags, base, far_half, far_rest, key_out, value_out):
    first = flags[2] == 0
    at_hub = flags[5] > 0
    tall = 64
    for begin in range(0, key_out.shape[0], tall):
        rows = pl.ds(begin, tall)
        half, rest = far_half[rows, :], far_rest[rows, :]
        far_key = jnp.where(first, half, rest).astype(F32)
        far_value = jnp.where(first, rest, half).astype(F32)
        far_key = jnp.where(at_hub, far_key, 0.0)
        far_value = jnp.where(at_hub, far_value, 0.0)
        key_out[rows, :] = (base[0, rows].astype(F32) + far_key).astype(BF16)
        value_out[rows, :] = (base[1, rows].astype(F32) + far_value).astype(BF16)


def across(shape, start=0):
    lead = (0,) * (len(shape) - 1)
    return pl.BlockSpec(tuple(shape[:-1]) + (SPAN,), lambda i, flags: lead + (i + start,))


def call(body, flags, ins, outs, steps, flops, name, aliases={}):
    shapes = [jax.ShapeDtypeStruct(s, t) for s, t, _ in outs]
    arrays = [a for a, _ in ins]
    moved = sum(a.size * a.dtype.itemsize for a in arrays + shapes)
    return pl.pallas_call(
        body,
        grid_spec=pltpu.PrefetchScalarGridSpec(
            num_scalar_prefetch=1,
            grid=(steps,),
            in_specs=[p or across(a.shape) for a, p in ins],
            out_specs=[p or across(s) for s, _, p in outs],
        ),
        out_shape=shapes,
        compiler_params=pltpu.CompilerParams(vmem_limit_bytes=56 * 1024 * 1024),
        cost_estimate=pl.CostEstimate(flops=flops, bytes_accessed=moved, transcendentals=0),
        input_output_aliases=aliases,
        name=name,
    )(flags, *arrays)


def place(z, x, c):
    return (z % NZ) * NX * NC + (x % NX) * NC + c % NC


def spots():
    return [(z, x, c) for z in range(NZ) for x in range(NX) for c in range(NC)]


def hop(dx=0, dc=0):
    return [(place(z, x, c), place(z, x + dx, c + dc)) for z, x, c in spots()]


Z_GROUPS = [[place(z, x, c) for z in range(NZ)] for x in range(NX) for c in range(NC)]


def send(value, pairs):
    return lax.ppermute(value, "region", pairs)


def pick(value, index):
    return lax.dynamic_index_in_dim(value, index, 0, keepdims=False)


def swap_z(value):
    return lax.all_to_all(value, "region", 0, 0, axis_index_groups=Z_GROUPS, tiled=True)


PLANE_GROUPS = [[place(z, x, c) for x in range(NX) for z in range(NZ)] for c in range(NC)]


def gather_plane(value):
    count = NZ * NX
    out = lax.all_to_all(
        jnp.broadcast_to(value[None], (count,) + value.shape),
        "region",
        0,
        0,
        axis_index_groups=PLANE_GROUPS,
        tiled=True,
    )
    return out.reshape((-1,) + value.shape[1:])


CORE = hop(dc=1)
CHIP = [p for r in range(1, NZ * NX * NC - 1, NC) for p in ((r, r + 1), (r + 1, r))]


def on_device(query, key_in, value, d_out, out_weight, attended, counts):
    region = lax.axis_index("region")
    x, c = (region // NC) % NX, region % NC
    first = c == 0
    query, key, value, grad_out = query[0], key_in[0], value[0], d_out[0]
    rows, width = query.shape
    quarter, eighth = rows // NX, rows // (NX * NZ)
    spots_count = NZ * NX * NC
    ids, flags, pair, *pieces = simple(
        prepare,
        [jnp.reshape(region, (1,)), attended, counts, key, value],
        [((spots_count, 1, 128), jnp.int32), ((8,), jnp.int32), ((2, rows, width), BF16)]
        + [((2, quarter, width), BF16)] * NX,
        "prepare",
        3,
    )
    arrived = [pieces[0]] + [send(pieces[k], hop(dx=k)) for k in range(1, NX)]
    ids = lax.all_to_all(ids, "region", 0, 0, tiled=True)
    mine, other, flags = simple(
        choose,
        [flags, ids, *arrived],
        [((quarter, width), BF16)] * 2 + [((8,), jnp.int32)],
        "choose",
        1,
    )
    part = jnp.where(flags[7] > 0, mine, send(other, hop(dc=1)))
    part, pair = lax.optimization_barrier((part, pair))
    near = [pair, send(pair, CORE), send(pair, CHIP)]
    share = pick(swap_z(part.reshape(NZ, eighth, width)), flags[6])
    share, near = lax.optimization_barrier((share, near))

    flat, double = (rows, width), (2, rows, width)
    stats = call(
        local_forward,
        flags,
        [(a, None) for a in (query, *near)],
        [(flat, F32, None)] * 3,
        width // SPAN,
        int(5e9),
        "local_forward",
    )
    d_attn = lax.dot_general(
        grad_out, out_weight, (((1,), (1,)), ((), ())), preferred_element_type=F32
    ).astype(BF16)
    half, stats, d_attn = lax.optimization_barrier((gather_plane(share), stats, d_attn))
    rest = send(half, hop(dc=1))

    slab = width // (NZ * NX * NC)
    by_spot = (NX, NZ, slab, width)
    spot_block = pl.BlockSpec((NX, SPAN // 128, slab, width), lambda i, flags: (0, i, 0, 0))
    whole = pl.BlockSpec(flat, lambda i, flags: (0, 0))
    attn, lse, cen, dq_far, far_mine, far_other, kept, sent = call(
        hub_block,
        flags,
        [(a, None) for a in (query, d_attn, half, rest, *stats)] + [(grad_out, whole)],
        [(flat, t, None) for t in (BF16, F32, F32, F32, BF16, BF16)]
        + [(by_spot, F32, spot_block), (by_spot, BF16, spot_block)],
        width // SPAN,
        int(9e9),
        "hub_block",
    )

    received = send(far_other, CORE)
    turned = send(sent, CORE)
    layer = nn(attn, out_weight).astype(BF16)
    received, turned, layer = lax.optimization_barrier((received, turned, layer))
    stacked = (NX, quarter, width)
    pieces = simple(
        add_pieces,
        [flags, far_mine.reshape(stacked), received.reshape(stacked), kept, turned],
        [((quarter + NZ * slab, width), BF16)] * NX,
        "add_pieces",
        1,
    )
    pieces, lse = lax.optimization_barrier((pieces, lse))
    pieces = [pieces[0]] + [send(pieces[k], hop(dx=k)) for k in range(1, NX)]

    blocks = width // SPAN
    double = (2, rows, width)

    def backward(lse, done, begin, steps):
        ins = [(a, across(a.shape, begin)) for a in (query, d_attn, *near, lse, cen, dq_far)]
        outs = [(flat, BF16), (double, F32), (double, BF16), (double, BF16)]
        return call(
            local_backward_into if done else local_backward,
            flags,
            ins + [(a, pl.BlockSpec(memory_space=pl.ANY)) for a in done],
            [(s, t, across(s, begin)) for s, t in outs],
            steps,
            int(2e9) * steps,
            "local_backward",
            {1 + len(ins) + i: i for i in range(len(done))},
        )

    grads = backward(lse, [], 0, blocks - 1)
    pieces, grads, lse = lax.optimization_barrier((pieces, grads, lse))
    summed = sum(p.astype(F32) for p in pieces).astype(BF16)
    both = [summed[:quarter].reshape(NZ, eighth, width), summed[quarter:].reshape(NZ, slab, width)]
    both = swap_z(jnp.concatenate(both, axis=1))
    grads = backward(lse, grads, blocks - 1, 1)
    d_query, own, to_core, to_chip = grads
    from_chip = send(to_chip, CHIP)
    from_core = send(to_core, CORE)
    both, own = lax.optimization_barrier((both, own))
    total = jnp.sum(both[:, :eighth].astype(F32), axis=0).astype(BF16)
    weight = jnp.sum(both[:, eighth:].astype(F32), axis=0)

    far_half = gather_plane(total)
    dp = lax.axis_size("dp")
    shares = [
        lax.ppermute(weight, "dp", [(i, (i + k) % dp) for i in range(dp)]) for k in range(1, dp)
    ]
    base = (own + from_core.astype(F32) + from_chip.astype(F32)).astype(BF16)
    far_half, shares, base = lax.optimization_barrier((far_half, shares, base))
    d_weight = weight + sum(shares)
    far_rest = send(far_half, CORE)
    d_key, d_value = simple(
        combine,
        [flags, base, far_half, far_rest],
        [(flat, BF16)] * 2,
        "combine",
        1,
    )
    return layer[None], d_query[None], d_key[None], d_value[None], d_weight


def solution(mesh):
    rows = P("dp", "region", None)
    return jax.shard_map(
        on_device,
        mesh=mesh,
        in_specs=(rows, rows, rows, rows, P(), P("region", None), P("region")),
        out_specs=(rows, rows, rows, rows, P("region", None)),
        check_vma=False,
    )
```

```python
import jax
import jax.numpy as jnp
from jax import lax
from jax.experimental import pallas as pl
from jax.experimental.pallas import tpu as pltpu
from jax.sharding import PartitionSpec as P

HEAD_DIM = 64
NZ, NX, NC = 8, 4, 2
SPAN = 256
F32 = jnp.float32
BF16 = jnp.bfloat16
NEVER = -1e30


def nt(a, b):
    return lax.dot_general(a, b, (((1,), (1,)), ((), ())), preferred_element_type=F32)


def tn(a, b):
    return lax.dot_general(a, b, (((0,), (0,)), ((), ())), preferred_element_type=F32)


def nn(a, b):
    return lax.dot_general(a, b, (((1,), (0,)), ((), ())), preferred_element_type=F32)


def half_masks(shape):
    lane = lax.broadcasted_iota(jnp.int32, shape, 1)
    return [lane < HEAD_DIM, lane >= HEAD_DIM]


def local_forward(flags, q, own, core, chip_key, chip_value, m_out, l_out, o_out):
    seen = [None, flags[0] > 0, flags[1] > 0]
    for g in range(SPAN // 128):
        cols = pl.ds(g * 128, 128)
        queries = q[:, cols] * 0.125
        masks = half_masks(queries.shape)
        keys = [own[0, :, cols], core[0, :, cols], chip_key[:, cols]]
        vals = [own[1, :, cols], core[1, :, cols], chip_value[:, cols]]
        tops, sums, mixes = [], [], []
        for mask in masks:
            part = jnp.where(mask, queries, 0).astype(BF16)
            scores = [nt(part, k) for k in keys]
            tops_of = [jnp.max(s, axis=1, keepdims=True) for s in scores]
            top = tops_of[0]
            for t, f in zip(tops_of[1:], seen[1:]):
                top = jnp.maximum(top, jnp.where(f, t, NEVER))
            shifts = [top if f is None else jnp.where(f, top, -NEVER) for f in seen]
            weights = [jnp.exp(s - t) for s, t in zip(scores, shifts)]
            sums.append(jnp.sum(weights[0] + weights[1] + weights[2], axis=1, keepdims=True))
            tops.append(top)
            mixes.append(sum(nn(w.astype(BF16), v) for w, v in zip(weights, vals)))
        m_out[:, cols] = jnp.where(masks[0], tops[0], tops[1])
        l_out[:, cols] = jnp.where(masks[0], sums[0], sums[1])
        o_out[:, cols] = jnp.where(masks[0], mixes[0], mixes[1])


def hub_block(
    flags, q, d, half, rest, m_in, l_in, o_in, grad,
    attn_out, lse_out, cen_out, dq_out, mine_out, other_out, kept_out, sent_out,
):
    first = flags[2] == 0
    seen = flags[3] > 0
    for g in range(SPAN // 128):
        cols = pl.ds(g * 128, 128)
        queries = q[:, cols] * 0.125
        grads = d[:, cols]
        masks = half_masks(queries.shape)
        a, b = half[:, cols], rest[:, cols]
        key = jnp.where(first, a, b)
        val = jnp.where(first, b, a)
        m_loc, l_loc, o_loc = m_in[:, cols], l_in[:, cols], o_in[:, cols]
        lses, cens, mixes, dqs = [], [], [], []
        dk = dv = 0.0
        for h, mask in enumerate(masks):
            part = jnp.where(mask, queries, 0).astype(BF16)
            gpart = jnp.where(mask, grads, 0).astype(BF16)
            at = slice(h * HEAD_DIM, h * HEAD_DIM + 1)
            scores = nt(part, key)
            old = m_loc[:, at]
            top = jnp.max(scores, axis=1, keepdims=True)
            top = jnp.maximum(old, jnp.where(seen, top, NEVER))
            weights = jnp.exp(scores - jnp.where(seen, top, -NEVER))
            fade = jnp.exp(old - top)
            total = l_loc[:, at] * fade + jnp.sum(weights, axis=1, keepdims=True)
            inv = 1.0 / total
            coarse = weights.astype(BF16)
            mix = (o_loc * fade + nn(coarse, val)) * inv
            cen = jnp.sum(mix * gpart.astype(F32), axis=1, keepdims=True)
            dscore = (weights * (nt(gpart, val) - cen)).astype(BF16)
            dqs.append(nn(dscore, key) * inv)
            dk += tn(dscore, (part.astype(F32) * inv).astype(BF16))
            dv += tn(coarse, (gpart.astype(F32) * inv).astype(BF16))
            lses.append(top + jnp.log(total))
            cens.append(cen)
            mixes.append(mix)
        attn = jnp.where(masks[0], mixes[0], mixes[1]).astype(BF16)
        attn_out[:, cols] = attn
        weight = tn(attn, grad[...])
        slab = weight.shape[0] // (NX * NC)
        weight = weight.reshape(NX, NC, slab, weight.shape[1])
        for j in range(NX):
            slot = (j - flags[4] + NX) % NX
            kept_out[slot, g] = jnp.where(first, weight[j, 0], weight[j, 1])
            sent_out[slot, g] = jnp.where(first, weight[j, 1], weight[j, 0]).astype(BF16)
        lse_out[:, cols] = jnp.where(masks[0], lses[0], lses[1])
        cen_out[:, cols] = jnp.where(masks[0], cens[0], cens[1])
        dq_out[:, cols] = jnp.where(masks[0], dqs[0], dqs[1])
        mine_out[:, cols] = jnp.where(first, dk, dv).astype(BF16)
        other_out[:, cols] = jnp.where(first, dv, dk).astype(BF16)


def local_backward(
    flags, q, d, own, core, chip_key, chip_value, lse_in, cen_in, dq_in,
    dq_out, own_out, core_out, chip_out,
):
    seen = [None, flags[0] > 0, flags[1] > 0]
    for g in range(SPAN // 128):
        cols = pl.ds(g * 128, 128)
        queries = q[:, cols] * 0.125
        grads = d[:, cols]
        masks = half_masks(queries.shape)
        keys = [own[0, :, cols], core[0, :, cols], chip_key[:, cols]]
        vals = [own[1, :, cols], core[1, :, cols], chip_value[:, cols]]
        lse, cens = lse_in[:, cols], cen_in[:, cols]
        parts = [jnp.where(m, queries, 0).astype(BF16) for m in masks]
        gparts = [jnp.where(m, grads, 0).astype(BF16) for m in masks]
        dq = [0.0, 0.0]
        for key, val, flag, out in zip(keys, vals, seen, (own_out, core_out, chip_out)):
            dk = dv = 0.0
            for h in range(2):
                at = slice(h * HEAD_DIM, h * HEAD_DIM + 1)
                shift = lse[:, at]
                if flag is not None:
                    shift = jnp.where(flag, shift, -NEVER)
                probs = jnp.exp(nt(parts[h], key) - shift)
                dscore = (probs * (nt(gparts[h], val) - cens[:, at])).astype(BF16)
                dq[h] += nn(dscore, key)
                dk += tn(dscore, parts[h])
                dv += tn(probs.astype(BF16), gparts[h])
            out[0, :, cols] = dk.astype(out.dtype)
            out[1, :, cols] = dv.astype(out.dtype)
        total = jnp.where(masks[0], dq[0], dq[1]) + dq_in[:, cols]
        dq_out[:, cols] = (total * 0.125).astype(BF16)


def prepare(spot, listed, counts, key, value, ids_out, flags_out, pair, *pieces):
    region = spot[0]
    left = right = far = jnp.int32(0)
    hub = jnp.int32(-1)
    for j in range(1, listed.shape[1]):
        entry = listed[0, j]
        used = j < counts[0]
        on_left, on_right = entry == region - 1, entry == region + 1
        beside = on_left | on_right
        left = jnp.where(used & on_left, 1, left)
        right = jnp.where(used & on_right, 1, right)
        far = jnp.where(used & jnp.logical_not(beside), 1, far)
        hub = jnp.where(used & jnp.logical_not(beside), entry, hub)
    x = region // NC % NX
    lower = region % NC == 0
    flags_out[0] = jnp.where(lower, right, left)
    flags_out[1] = jnp.where(lower, left, right)
    flags_out[2] = region % NC
    flags_out[3] = far
    flags_out[4] = x
    flags_out[5] = region
    flags_out[6] = 0
    flags_out[7] = 0
    ids_out[...] = jnp.full(ids_out.shape, hub, jnp.int32)
    pair[0] = key[...]
    pair[1] = value[...]
    quarter = pieces[0].shape[1]
    for k, out in enumerate(pieces):
        rows = pl.ds(pl.multiple_of((x + k) % NX * quarter, quarter), quarter)
        out[0] = key[rows, :]
        out[1] = value[rows, :]


def add_pieces(flags, mine, theirs, kept, turned, *pieces):
    quarter = mine.shape[1]
    for k, out in enumerate(pieces):
        spot = (flags[4] + k) % NX
        far = mine[spot].astype(F32) + theirs[spot].astype(F32)
        out[pl.ds(0, quarter), :] = far.astype(BF16)
        slab = kept[k] + turned[k].astype(F32)
        slab = slab.reshape(-1, slab.shape[-1]).astype(BF16)
        out[pl.ds(quarter, slab.shape[0]), :] = slab


def simple(body, ins, outs, name, scalars=0):
    smem = pl.BlockSpec(memory_space=pltpu.SMEM)
    vmem = pl.BlockSpec(memory_space=pltpu.VMEM)
    return pl.pallas_call(
        body,
        in_specs=[smem] * scalars + [vmem] * (len(ins) - scalars),
        out_specs=[smem if s == (8,) else vmem for s, _ in outs],
        out_shape=[jax.ShapeDtypeStruct(s, t) for s, t in outs],
        compiler_params=pltpu.CompilerParams(vmem_limit_bytes=32 * 1024 * 1024),
        name=name,
    )(*ins)


def local_backward_into(flags, *refs):
    local_backward(flags, *refs[:9], *refs[13:])


def choose(flags, ids, own, one, two, three, mine_out, other_out, flags_out):
    hub = jnp.max(ids[...])
    c, x = flags[2], flags[4]
    hub_z, hub_x, hub_c = hub // (NX * NC), hub // NC % NX, hub % NC
    for i in range(5):
        flags_out[i] = flags[i]
    flags_out[5] = (hub == flags[5]).astype(jnp.int32)
    flags_out[6] = hub_z
    flags_out[7] = (hub_c == c).astype(jnp.int32)
    for k, ref in enumerate((own, one, two, three)):

        @pl.when((x - hub_x + NX) % NX == k)
        def _():
            mine_out[...] = ref[c]
            other_out[...] = ref[1 - c]


def combine(flags, base, far_half, far_rest, key_out, value_out):
    first = flags[2] == 0
    at_hub = flags[5] > 0
    tall = 64
    for begin in range(0, key_out.shape[0], tall):
        rows = pl.ds(begin, tall)
        half, rest = far_half[rows, :], far_rest[rows, :]
        far_key = jnp.where(first, half, rest).astype(F32)
        far_value = jnp.where(first, rest, half).astype(F32)
        far_key = jnp.where(at_hub, far_key, 0.0)
        far_value = jnp.where(at_hub, far_value, 0.0)
        key_out[rows, :] = (base[0, rows].astype(F32) + far_key).astype(BF16)
        value_out[rows, :] = (base[1, rows].astype(F32) + far_value).astype(BF16)


def across(shape, start=0):
    lead = (0,) * (len(shape) - 1)
    return pl.BlockSpec(tuple(shape[:-1]) + (SPAN,), lambda i, flags: lead + (i + start,))


def call(body, flags, ins, outs, steps, flops, name, aliases={}):
    shapes = [jax.ShapeDtypeStruct(s, t) for s, t, _ in outs]
    arrays = [a for a, _ in ins]
    moved = sum(a.size * a.dtype.itemsize for a in arrays + shapes)
    return pl.pallas_call(
        body,
        grid_spec=pltpu.PrefetchScalarGridSpec(
            num_scalar_prefetch=1,
            grid=(steps,),
            in_specs=[p or across(a.shape) for a, p in ins],
            out_specs=[p or across(s) for s, _, p in outs],
        ),
        out_shape=shapes,
        compiler_params=pltpu.CompilerParams(vmem_limit_bytes=56 * 1024 * 1024),
        cost_estimate=pl.CostEstimate(flops=flops, bytes_accessed=moved, transcendentals=0),
        input_output_aliases=aliases,
        name=name,
    )(flags, *arrays)


def place(z, x, c):
    return (z % NZ) * NX * NC + (x % NX) * NC + c % NC


def spots():
    return [(z, x, c) for z in range(NZ) for x in range(NX) for c in range(NC)]


def hop(dx=0, dc=0):
    return [(place(z, x, c), place(z, x + dx, c + dc)) for z, x, c in spots()]


Z_GROUPS = [[place(z, x, c) for z in range(NZ)] for x in range(NX) for c in range(NC)]


def send(value, pairs):
    return lax.ppermute(value, "region", pairs)


def pick(value, index):
    return lax.dynamic_index_in_dim(value, index, 0, keepdims=False)


def swap_z(value):
    return lax.all_to_all(value, "region", 0, 0, axis_index_groups=Z_GROUPS, tiled=True)


PLANE_GROUPS = [[place(z, x, c) for x in range(NX) for z in range(NZ)] for c in range(NC)]


def gather_plane(value):
    count = NZ * NX
    out = lax.all_to_all(
        jnp.broadcast_to(value[None], (count,) + value.shape),
        "region",
        0,
        0,
        axis_index_groups=PLANE_GROUPS,
        tiled=True,
    )
    return out.reshape((-1,) + value.shape[1:])


CORE = hop(dc=1)
CHIP = [p for r in range(1, NZ * NX * NC - 1, NC) for p in ((r, r + 1), (r + 1, r))]


def on_device(query, key_in, value, d_out, out_weight, attended, counts):
    region = lax.axis_index("region")
    x, c = (region // NC) % NX, region % NC
    first = c == 0
    query, key, value, grad_out = query[0], key_in[0], value[0], d_out[0]
    rows, width = query.shape
    quarter, eighth = rows // NX, rows // (NX * NZ)
    spots_count = NZ * NX * NC
    ids, flags, pair, *pieces = simple(
        prepare,
        [jnp.reshape(region, (1,)), attended, counts, key, value],
        [((spots_count, 1, 128), jnp.int32), ((8,), jnp.int32), ((2, rows, width), BF16)]
        + [((2, quarter, width), BF16)] * NX,
        "prepare",
        3,
    )
    arrived = [pieces[0]] + [send(pieces[k], hop(dx=k)) for k in range(1, NX)]
    ids = lax.all_to_all(ids, "region", 0, 0, tiled=True)
    mine, other, flags = simple(
        choose,
        [flags, ids, *arrived],
        [((quarter, width), BF16)] * 2 + [((8,), jnp.int32)],
        "choose",
        1,
    )
    part = jnp.where(flags[7] > 0, mine, send(other, hop(dc=1)))
    part, pair, value = lax.optimization_barrier((part, pair, value))
    near = [pair, send(pair, CORE), send(key, CHIP), send(value, CHIP)]
    share = pick(swap_z(part.reshape(NZ, eighth, width)), flags[6])
    share, near = lax.optimization_barrier((share, near))

    flat, double = (rows, width), (2, rows, width)
    stats = call(
        local_forward,
        flags,
        [(a, None) for a in (query, *near)],
        [(flat, F32, None)] * 3,
        width // SPAN,
        int(5e9),
        "local_forward",
    )
    d_attn = lax.dot_general(
        grad_out, out_weight, (((1,), (1,)), ((), ())), preferred_element_type=F32
    ).astype(BF16)
    half, stats, d_attn = lax.optimization_barrier((gather_plane(share), stats, d_attn))
    rest = send(half, hop(dc=1))

    slab = width // (NZ * NX * NC)
    by_spot = (NX, NZ, slab, width)
    spot_block = pl.BlockSpec((NX, SPAN // 128, slab, width), lambda i, flags: (0, i, 0, 0))
    whole = pl.BlockSpec(flat, lambda i, flags: (0, 0))
    attn, lse, cen, dq_far, far_mine, far_other, kept, sent = call(
        hub_block,
        flags,
        [(a, None) for a in (query, d_attn, half, rest, *stats)] + [(grad_out, whole)],
        [(flat, t, None) for t in (BF16, F32, F32, F32, BF16, BF16)]
        + [(by_spot, F32, spot_block), (by_spot, BF16, spot_block)],
        width // SPAN,
        int(9e9),
        "hub_block",
    )

    received = send(far_other, CORE)
    turned = send(sent, CORE)
    layer = nn(attn, out_weight).astype(BF16)
    received, turned, layer = lax.optimization_barrier((received, turned, layer))
    stacked = (NX, quarter, width)
    pieces = simple(
        add_pieces,
        [flags, far_mine.reshape(stacked), received.reshape(stacked), kept, turned],
        [((quarter + NZ * slab, width), BF16)] * NX,
        "add_pieces",
        1,
    )
    pieces, lse = lax.optimization_barrier((pieces, lse))
    pieces = [pieces[0]] + [send(pieces[k], hop(dx=k)) for k in range(1, NX)]

    blocks = width // SPAN
    double = (2, rows, width)

    def backward(lse, done, begin, steps):
        ins = [(a, across(a.shape, begin)) for a in (query, d_attn, *near, lse, cen, dq_far)]
        outs = [(flat, BF16), (double, F32), (double, BF16), (double, BF16)]
        return call(
            local_backward_into if done else local_backward,
            flags,
            ins + [(a, pl.BlockSpec(memory_space=pl.ANY)) for a in done],
            [(s, t, across(s, begin)) for s, t in outs],
            steps,
            int(2e9) * steps,
            "local_backward",
            {1 + len(ins) + i: i for i in range(len(done))},
        )

    grads = backward(lse, [], 0, blocks - 1)
    pieces, grads, lse = lax.optimization_barrier((pieces, grads, lse))
    summed = sum(p.astype(F32) for p in pieces).astype(BF16)
    both = [summed[:quarter].reshape(NZ, eighth, width), summed[quarter:].reshape(NZ, slab, width)]
    both = swap_z(jnp.concatenate(both, axis=1))
    grads = backward(lse, grads, blocks - 1, 1)
    d_query, own, to_core, to_chip = grads
    from_chip = send(to_chip, CHIP)
    from_core = send(to_core, CORE)
    both, own = lax.optimization_barrier((both, own))
    total = jnp.sum(both[:, :eighth].astype(F32), axis=0).astype(BF16)
    weight = jnp.sum(both[:, eighth:].astype(F32), axis=0)

    far_half = gather_plane(total)
    dp = lax.axis_size("dp")
    shares = [
        lax.ppermute(weight, "dp", [(i, (i + k) % dp) for i in range(dp)]) for k in range(1, dp)
    ]
    base = (own + from_core.astype(F32) + from_chip.astype(F32)).astype(BF16)
    far_half, shares, base = lax.optimization_barrier((far_half, shares, base))
    d_weight = weight + sum(shares)
    far_rest = send(far_half, CORE)
    d_key, d_value = simple(
        combine,
        [flags, base, far_half, far_rest],
        [(flat, BF16)] * 2,
        "combine",
        1,
    )
    return layer[None], d_query[None], d_key[None], d_value[None], d_weight


def solution(mesh):
    rows = P("dp", "region", None)
    return jax.shard_map(
        on_device,
        mesh=mesh,
        in_specs=(rows, rows, rows, rows, P(), P("region", None), P("region")),
        out_specs=(rows, rows, rows, rows, P("region", None)),
        check_vma=False,
    )
```
